32 devices in a mesh: segment: 4 (over y, x), graph: 8 (over z, core).
Axes of the slice: x: 2, y: 2, z: 4, core: 2. Of those that a mesh axis runs over, the one named last changes fastest.
Arguments:
- features: bfloat16 [4096, 1024], P('graph'), may hold values from -6 to 6
- weights: bfloat16 [8, 1024, 1024], P(None, 'graph'), may hold values from -0.25 to 0.25
- history: bfloat16 [8, 512, 1024], P(None, 'graph'), may hold values from 0 to 1.1953125
- own_adj: bfloat16 [4, 1024, 128], P(None, 'graph'), may hold values from 0 to 0.00390625
- side_adj: bfloat16 [4, 4, 128, 128], P(None, None, 'graph'), may hold values from 0 to 0.012451172
- hist_adj: bfloat16 [4, 512, 128], P(None, 'graph'), may hold values from 0 to 0.009338379
- send_ids: int32 [4, 4, 128], P(None, None, 'graph'), may hold values from 0 to 127, as said below
- hist_ids: int32 [4, 512], P(None, 'graph'), may hold values from 0 to 63
Outputs:
- layer_out: bfloat16 [8, 4096, 1024], P('segment', 'graph')
The draws below stay inside these ranges and needn't reach their ends.
Inputs may be any that keep to these rules, and one draw needn't show every extreme that they name: `send_ids`: each list of 16 row numbers for one batch, one partition and one direction has distinct entries.
All inputs are finite; a program needn't handle non-finite values.
Results may differ from the reference program's by a relative error of at most 0.0032.
Values may be sent and summed in bfloat16 or wider, within the bound.
A program may use at most 64 MiB of HBM per device.

```python
import jax
import jax.numpy as jnp

F = 1024
LAYERS = 8
BATCHES = 4
BR = 128
EDGE_ROWS = 16
HIST_SEL = 64
HIST_ROWS = 64
VERTS = 4096
BR_ALL = 1024
SEND_ALL = 128
HSEL_ALL = 512
HIST_ALL = 512
N_GRAPH = 8


def draw_send_ids(key, part):
    list_count = BATCHES * 4 * (SEND_ALL // EDGE_ROWS)
    subkeys = jax.random.split(jax.random.fold_in(key, 7), list_count)
    chosen = jax.vmap(lambda single: jax.random.permutation(single, BR)[:EDGE_ROWS])(subkeys)
    return chosen.astype(jnp.int32).reshape(BATCHES, 4, SEND_ALL)


def place_ends(result, own_key, low, largest):
    place = [jax.random.randint(jax.random.fold_in(own_key, axis), (), 0, length) for axis, length in enumerate(result.shape)]
    widest = result.shape.index(max(result.shape))
    neighbour = place[:widest] + [(place[widest] + 1) % result.shape[widest]] + place[widest + 1:]
    return result.at[tuple(place)].set(low).at[tuple(neighbour)].set(largest)


def with_spikes(drawn, stream_key, source, target, blocks, factor):
    def block_of(axis_at):
        return (jnp.arange(drawn.shape[axis_at]) // (drawn.shape[axis_at] // blocks)).reshape((-1,) + (1,) * (drawn.ndim - 1 - axis_at))

    first = jax.random.permutation(stream_key, blocks)[block_of(target)]
    second = (block_of(target) + blocks // 2) % blocks
    return jnp.where((block_of(source) == first) | (block_of(source) == second), factor * drawn, drawn)


def shard_levels(stream_key, dims, cuts, smallest, high):
    def one(axis_at, shards_of):
        heights = jax.random.uniform(jax.random.fold_in(jax.random.fold_in(stream_key, 6), axis_at), (shards_of,), jnp.float32, smallest / len(cuts), high / len(cuts))
        return jnp.repeat(jnp.exp(heights), dims[axis_at] // shards_of).reshape((-1,) + (1,) * (len(dims) - axis_at - 1))

    loudness = one(*cuts[0])
    for cut in cuts[1:]:
        loudness = loudness * one(*cut)
    return loudness


def noise(rng, extent, width, reach, pieces=(), kind=jnp.bfloat16):
    array = width * jax.random.normal(rng, extent, jnp.float32)
    if pieces:
        array = array * shard_levels(rng, extent, pieces, -0.22, 0.18)
    return jnp.clip(array, -reach, reach).astype(kind)


def gaussian_with(own_key, extent, width, most, cuts, heavy, kind=jnp.bfloat16):
    entries = width * jax.random.normal(own_key, extent, jnp.float32)
    if cuts:
        entries = entries * shard_levels(own_key, extent, cuts, -0.22, 0.18)
    return jnp.clip(with_spikes(entries, jax.random.fold_in(own_key, 3), *heavy), -most, most).astype(kind)


def setup_inputs(seed: int = 0) -> dict:
    arg_keys = jax.random.split(jax.random.key(seed), 9)
    features = noise(arg_keys[0], (VERTS, F), 1.0, 6.0, ((0, 8),))
    weights = gaussian_with(arg_keys[1], (LAYERS, F, F), F ** -0.5, 0.25, ((1, 8),), (1, 2, 8, 2.0))
    history = jnp.clip(1.1953125 * jax.random.uniform(arg_keys[2], (LAYERS, HIST_ALL, F), jnp.float32) ** shard_levels(arg_keys[2], (LAYERS, HIST_ALL, F), ((1, 8),), -0.2, 0.2), 0.0, 1.1953125).astype(jnp.bfloat16)
    own_adj = jnp.clip(0.00390625 * jax.random.uniform(arg_keys[3], (BATCHES, BR_ALL, BR), jnp.float32) ** shard_levels(arg_keys[3], (BATCHES, BR_ALL, BR), ((1, 8),), -0.2, 0.2), 0.0, 0.00390625).astype(jnp.bfloat16)
    side_adj = jnp.clip(0.012451172 * jax.random.uniform(arg_keys[4], (BATCHES, 4, SEND_ALL, BR), jnp.float32) ** shard_levels(arg_keys[4], (BATCHES, 4, SEND_ALL, BR), ((2, 8),), -0.2, 0.2), 0.0, 0.012451172).astype(jnp.bfloat16)
    hist_adj = jnp.clip(0.009338379 * jax.random.uniform(arg_keys[5], (BATCHES, HSEL_ALL, BR), jnp.float32) ** shard_levels(arg_keys[5], (BATCHES, HSEL_ALL, BR), ((1, 8),), -0.2, 0.2), 0.0, 0.009338379).astype(jnp.bfloat16)
    send_ids = draw_send_ids(jax.random.fold_in(arg_keys[8], 71), 0)
    hist_ids = place_ends(jax.random.randint(arg_keys[7], (BATCHES, HSEL_ALL), 0, HIST_ROWS), jax.random.fold_in(arg_keys[7], 1), 0, HIST_ROWS - 1).astype(jnp.int32)
    return dict(features=features, weights=weights, history=history, own_adj=own_adj, side_adj=side_adj, hist_adj=hist_adj, send_ids=send_ids, hist_ids=hist_ids)


ALPHA = 0.1
LAMBDA = 1.5
OFFSETS = (1, -1, 2, -2)


def displace(blocks, offset):
    padding = jnp.zeros((abs(offset),) + blocks.shape[1:], blocks.dtype)
    if offset > 0:
        return jnp.concatenate([padding, blocks[:-offset]], axis=0)
    return jnp.concatenate([blocks[-offset:], padding], axis=0)


def layer_step(current, initial, number, weight, tables, own_tile, side_tile, hist_tile, send_rows, past_rows):
    aggregate = jnp.einsum("pij,pjf->pif", own_tile.astype(jnp.float32), current.astype(jnp.float32))
    picked = jax.vmap(lambda source, chosen: source[chosen])(current, send_rows)
    for direction in range(4):
        arrived = displace(picked[:, direction], OFFSETS[direction])
        aggregate = aggregate + jnp.einsum("pri,prf->pif", side_tile[direction].astype(jnp.float32), arrived.astype(jnp.float32))
    looked = jax.vmap(lambda source, chosen: source[chosen])(tables[number], past_rows)
    aggregate = aggregate + jnp.einsum("pri,prf->pif", hist_tile.astype(jnp.float32), looked.astype(jnp.float32))
    support = (1.0 - ALPHA) * aggregate + ALPHA * initial.astype(jnp.float32)
    columns = support.shape[2]
    mixing = jnp.dot(support.astype(jnp.bfloat16).reshape(-1, columns), weight, preferred_element_type=jnp.float32).reshape(support.shape)
    strength = jnp.log(LAMBDA / (jnp.float32(number) + 1.0) + 1.0)
    return jax.nn.relu((1.0 - strength) * support + strength * mixing).astype(jnp.bfloat16)


def reference(features, weights, history, own_adj, side_adj, hist_adj, send_ids, hist_ids):
    columns = features.shape[1]
    inputs = features.reshape(N_GRAPH, BATCHES, BR, columns)
    tables = history.reshape(LAYERS, N_GRAPH, HIST_ROWS, columns)
    own_all = own_adj.reshape(BATCHES, N_GRAPH, BR, BR)
    side_all = side_adj.reshape(BATCHES, 4, N_GRAPH, EDGE_ROWS, BR)
    hist_all = hist_adj.reshape(BATCHES, N_GRAPH, HIST_SEL, BR)
    send_all = send_ids.reshape(BATCHES, 4, N_GRAPH, EDGE_ROWS).transpose(0, 2, 1, 3)
    past_all = hist_ids.reshape(BATCHES, N_GRAPH, HIST_SEL)
    collected = []
    for batch in range(BATCHES):
        initial = inputs[:, batch]
        current = initial
        produced = []
        for number in range(LAYERS):
            current = layer_step(current, initial, number, weights[number], tables, own_all[batch], side_all[batch], hist_all[batch], send_all[batch], past_all[batch])
            produced.append(current)
        collected.append(jnp.stack(produced))
    stacked = jnp.stack(collected, axis=1)
    return stacked.transpose(0, 2, 1, 3, 4).reshape(LAYERS, N_GRAPH * BATCHES * BR, columns)
```

```python
import math

import jax
import jax.numpy as jnp
from jax import lax
from jax.experimental import pallas as pl
from jax.experimental.pallas import tpu as pltpu
from jax.sharding import PartitionSpec as P

ALPHA = 0.1
LAMBDA = 1.5
OFFSETS = (1, -1, 2, -2)


def shifted(value, axis, steps):
    count = lax.axis_size(axis)
    initial, last = (max(0, -steps), min(count, count - steps))
    return lax.ppermute(value, axis, [(source, source + steps) for source in range(initial, last)])


def propagate(
    current, initial, layer_number, weight, tables, own_tile, side_tile, send_rows, past_rows
):
    edge_count = send_rows.shape[1]
    picked = jnp.take(current, send_rows.reshape(-1), axis=0)
    arrived = []
    for direction in range(len(OFFSETS)):
        outgoing = picked[direction * edge_count : (direction + 1) * edge_count]
        arrived.append(shifted(outgoing, "graph", OFFSETS[direction]))
    layer_table = lax.dynamic_index_in_dim(tables, layer_number, 0, keepdims=False)
    arrived.append(jnp.take(layer_table, past_rows, axis=0))
    gathered_rows = jnp.concatenate(arrived, axis=0)
    aggregate = jnp.dot(own_tile, current, preferred_element_type=jnp.float32)
    aggregate = aggregate + lax.dot_general(
        side_tile, gathered_rows, (((0,), (0,)), ((), ())), preferred_element_type=jnp.float32
    )
    support = (1.0 - ALPHA) * aggregate + ALPHA * initial.astype(jnp.float32)
    mixing = jnp.dot(support.astype(jnp.bfloat16), weight, preferred_element_type=jnp.float32)
    strength = jnp.log(LAMBDA / (layer_number.astype(jnp.float32) + 1.0) + 1.0)
    return jax.nn.relu((1.0 - strength) * support + strength * mixing).astype(jnp.bfloat16)


def batch_tiles(own_adj, side_adj, hist_adj, send_ids, hist_ids, batch_safe):
    batch_rows = own_adj.shape[2]
    side_edges = side_adj.shape[1] * side_adj.shape[2]
    own_tile = lax.dynamic_index_in_dim(own_adj, batch_safe, 0, keepdims=False)
    edge_tile = lax.dynamic_index_in_dim(side_adj, batch_safe, 0, keepdims=False).reshape(
        side_edges, batch_rows
    )
    past_tile = lax.dynamic_index_in_dim(hist_adj, batch_safe, 0, keepdims=False)
    side_tile = jnp.concatenate([edge_tile, past_tile], axis=0)
    send_rows = lax.dynamic_index_in_dim(send_ids, batch_safe, 0, keepdims=False)
    past_rows = lax.dynamic_index_in_dim(hist_ids, batch_safe, 0, keepdims=False)
    return (own_tile, side_tile, send_rows, past_rows)


def shards(features, weights, history, own_adj, side_adj, hist_adj, send_ids, hist_ids):
    segment_pos = lax.axis_index("segment")
    segment_count = lax.axis_size("segment")
    batch_count = own_adj.shape[0]
    batch_rows = own_adj.shape[2]
    layer_total = weights.shape[0]
    kept_slots = layer_total // segment_count
    initial = lax.dynamic_slice_in_dim(features, segment_pos * batch_rows, batch_rows, 0)
    own_tile, side_tile, send_rows, past_rows = batch_tiles(
        own_adj, side_adj, hist_adj, send_ids, hist_ids, segment_pos
    )
    current = initial
    produced = []
    for number in range(layer_total):
        weight = lax.all_gather(weights[number], "graph", axis=0, tiled=True)
        current = propagate(
            current,
            initial,
            jnp.int32(number),
            weight,
            history,
            own_tile,
            side_tile,
            send_rows,
            past_rows,
        )
        produced.append(current)
    arranged = jnp.stack(
        [
            jnp.stack([produced[kept_slots * target + slot] for target in range(segment_count)])
            for slot in range(kept_slots)
        ]
    )
    received = lax.all_to_all(arranged, "segment", split_axis=1, concat_axis=1, tiled=True)
    return received.reshape(kept_slots, batch_count * batch_rows, features.shape[1])


TILE_ROWS = 16
MESH = pl.DeviceIdType.MESH


def column_of(row):
    count = row.shape[1]
    down = lax.broadcasted_iota(jnp.int32, (count, count), 0)
    across = lax.broadcasted_iota(jnp.int32, (count, count), 1)
    spread = jnp.broadcast_to(row.astype(jnp.float32), (count, count))
    return jnp.sum(jnp.where(down == across, spread, 0.0), axis=1, keepdims=True)


def selector(row, width):
    across = lax.broadcasted_iota(jnp.int32, (row.shape[1], width), 1).astype(jnp.float32)
    return jnp.where(across == column_of(row), 1.0, 0.0).astype(jnp.bfloat16)


def transposed_dot(left, right):
    return lax.dot_general(
        left, right, (((0,), (0,)), ((), ())), preferred_element_type=jnp.float32
    )


def stage_kernel(
    segments, places, layer_total,
    features, weights, history, own_adj, side_adj, hist_adj, send_ids, hist_ids,
    out,
    full, base, select, entering, leaving, arrived,
    own_sem, full_recv, up_send, down_send, pair_send,
    edge_send, edge_recv, hop_send, hop_recv,
):
    seg = lax.axis_index("segment")
    me = lax.axis_index("graph")
    kept = layer_total // segments
    batches, rows = own_adj.shape[0], own_adj.shape[2]
    shard = weights.shape[1]
    edge = send_ids.shape[2]
    chips = places // 2
    chip = me // 2
    core = me % 2
    pair = me + 1 - 2 * core
    first_layer = seg * kept

    barrier = pltpu.get_barrier_semaphore()
    expected = jnp.int32(0)
    for offset in OFFSETS:
        there = me + offset
        inside = jnp.logical_and(there >= 0, there < places)

        @pl.when(inside)
        def _():
            pl.semaphore_signal(barrier, inc=1, device_id={"graph": there}, device_id_type=MESH)

        expected = expected + inside.astype(jnp.int32)
    for step in (1, -1):
        beside = seg + step
        inside = jnp.logical_and(beside >= 0, beside < segments)

        @pl.when(inside)
        def _():
            pl.semaphore_signal(
                barrier, inc=1, device_id={"segment": beside}, device_id_type=MESH
            )

        expected = expected + inside.astype(jnp.int32)
    pl.semaphore_wait(barrier, expected)

    def block(slot, owner):
        return full.at[slot, pl.ds(pl.multiple_of(owner * shard, shard), shard)]

    def push(slot, owner, source, target, send_sem):
        return pltpu.make_async_remote_copy(
            src_ref=source,
            dst_ref=block(slot, owner),
            send_sem=send_sem.at[slot, owner // 2],
            recv_sem=full_recv.at[slot, owner],
            device_id={"graph": target},
            device_id_type=MESH,
        )

    def landed(slot, owner):
        push(slot, owner, block(slot, owner), pair, pair_send).wait_recv()

    def own_copy(slot):
        return pltpu.make_async_copy(
            weights.at[first_layer + slot], block(slot, me), own_sem.at[slot]
        )

    def open_slot(slot):
        source = weights.at[first_layer + slot]

        @pl.when(chip < chips - 1)
        def _():
            push(slot, me, source, me + 2, up_send).start()

        @pl.when(chip > 0)
        def _():
            push(slot, me, source, me - 2, down_send).start()

        push(slot, me, source, pair, pair_send).start()
        own_copy(slot).start()

    def relay(slot, distance):
        below = me - 2 * distance

        @pl.when(below >= 0)
        def _():
            landed(slot, below)

            @pl.when(chip < chips - 1)
            def _():
                push(slot, below, block(slot, below), me + 2, up_send).start()

            push(slot, below, block(slot, below), pair, pair_send).start()

        above = me + 2 * distance

        @pl.when(above < places)
        def _():
            landed(slot, above)

            @pl.when(chip > 0)
            def _():
                push(slot, above, block(slot, above), me - 2, down_send).start()

            push(slot, above, block(slot, above), pair, pair_send).start()

    def close_slot(slot):
        own_copy(slot).wait()

        def from_pair(other, carry):
            landed(slot, 2 * other + 1 - core)
            return carry

        lax.fori_loop(0, chips, from_pair, 0)

    def edge_copy(slot, batch, direction):
        part = pl.ds(direction * edge, edge)
        return pltpu.make_async_remote_copy(
            src_ref=leaving.at[slot, batch, part],
            dst_ref=arrived.at[slot, batch, part],
            send_sem=edge_send.at[slot, batch, direction],
            recv_sem=edge_recv.at[slot, batch, direction],
            device_id={"graph": me + OFFSETS[direction]},
            device_id_type=MESH,
        )

    def sends(direction):
        there = me + OFFSETS[direction]
        return jnp.logical_and(there >= 0, there < places)

    def receives(direction):
        there = me - OFFSETS[direction]
        return jnp.logical_and(there >= 0, there < places)

    def send_edges(slot, batch, current):
        leaving[slot, batch] = jnp.dot(
            select[batch], current, preferred_element_type=jnp.float32
        ).astype(jnp.bfloat16)
        for direction in range(len(OFFSETS)):

            @pl.when(sends(direction))
            def _():
                edge_copy(slot, batch, direction).start()

    def batch_range(batch):
        return pl.ds(pl.multiple_of(batch * rows, rows), rows)

    def hop(batch):
        return pltpu.make_async_remote_copy(
            src_ref=out.at[kept - 1, batch_range(batch)],
            dst_ref=entering.at[batch],
            send_sem=hop_send.at[batch],
            recv_sem=hop_recv.at[batch],
            device_id={"segment": seg + 1},
            device_id_type=MESH,
        )

    def prepare(batch, carry):
        for direction in range(len(OFFSETS)):
            part = pl.ds(direction * edge, edge)
            select[batch, part] = selector(
                send_ids[batch, pl.ds(direction, 1), :], rows
            )
            for slot in range(kept):

                @pl.when(jnp.logical_not(receives(direction)))
                def _():
                    arrived[slot, batch, part] = jnp.zeros(
                        (edge, arrived.shape[3]), jnp.bfloat16
                    )

        initial = features[batch_range(batch), :]

        @pl.when(seg == 0)
        def _():
            entering[batch] = initial

        lookup = selector(hist_ids[pl.ds(batch, 1), :], history.shape[1])
        for slot in range(kept):
            looked = jnp.dot(
                lookup, history[first_layer + slot], preferred_element_type=jnp.float32
            ).astype(jnp.bfloat16)
            past = transposed_dot(hist_adj[batch], looked)
            base[slot, batch] = (1.0 - ALPHA) * past + ALPHA * initial.astype(jnp.float32)
        return carry

    def layer(slot, batch):
        strength = jnp.float32(0.0)
        for number in range(layer_total):
            value = math.log(LAMBDA / (number + 1.0) + 1.0)
            strength = jnp.where(first_layer + slot == number, jnp.float32(value), strength)
        if slot == 0:
            current = entering[batch]
        else:
            current = out[slot - 1, batch_range(batch), :]
        aggregate = jnp.dot(own_adj[batch], current, preferred_element_type=jnp.float32)
        for direction in range(len(OFFSETS)):

            @pl.when(receives(direction))
            def _():
                edge_copy(slot, batch, direction).wait_recv()

        aggregate = aggregate + transposed_dot(side_adj[batch], arrived[slot, batch])
        support = (1.0 - ALPHA) * aggregate + base[slot, batch]
        mixing = jnp.dot(
            support.astype(jnp.bfloat16), full[slot], preferred_element_type=jnp.float32
        )
        result = jnp.maximum((1.0 - strength) * support + strength * mixing, 0.0)
        result = result.astype(jnp.bfloat16)
        out[slot, batch_range(batch), :] = result
        if slot < kept - 1:
            send_edges(slot + 1, batch, result)
        else:

            @pl.when(seg < segments - 1)
            def _():
                hop(batch).start()

    open_slot(0)
    lax.fori_loop(0, batches, prepare, 0)
    for slot in range(kept):
        for distance in range(1, chips):
            relay(slot, distance)
            if slot < kept - 1 and distance == max(1, chips - 2):
                open_slot(slot + 1)
    for slot in range(kept):
        close_slot(slot)

    def tick(time, carry):
        @pl.when(time < batches)
        def _():
            @pl.when(seg > 0)
            def _():
                hop(time).wait_recv()

            send_edges(0, time, entering[time])

        for slot in range(kept - 1, -1, -1):
            batch = time - slot

            @pl.when(jnp.logical_and(batch >= 0, batch < batches))
            def _():
                layer(slot, batch)

        return carry

    lax.fori_loop(0, batches + kept - 1, tick, 0)

    def finish(batch, carry):
        for slot in range(kept):
            for direction in range(len(OFFSETS)):

                @pl.when(sends(direction))
                def _():
                    edge_copy(slot, batch, direction).wait_send()

        @pl.when(seg < segments - 1)
        def _():
            hop(batch).wait_send()

        return carry

    lax.fori_loop(0, batches, finish, 0)

    def drain(other, carry):
        owner = 2 * other + core
        for slot in range(kept):
            push(slot, owner, block(slot, owner), pair, pair_send).wait_send()

            @pl.when(jnp.logical_and(other <= chip, chip < chips - 1))
            def _():
                push(slot, owner, block(slot, owner), me + 2, up_send).wait_send()

            @pl.when(jnp.logical_and(other >= chip, chip > 0))
            def _():
                push(slot, owner, block(slot, owner), me - 2, down_send).wait_send()

        return carry

    lax.fori_loop(0, chips, drain, 0)


def staged(features, weights, history, own_adj, side_adj, hist_adj, send_ids, hist_ids):
    segments = lax.axis_size("segment")
    places = lax.axis_size("graph")
    layer_total, shard, width = weights.shape
    kept = layer_total // segments
    batches, rows = own_adj.shape[0], own_adj.shape[2]
    edges = side_adj.shape[1] * side_adj.shape[2]
    chips = places // 2
    dma = pltpu.SemaphoreType.DMA

    def kernel(*refs):
        stage_kernel(segments, places, layer_total, *refs)

    vmem = pl.BlockSpec(memory_space=pltpu.VMEM)
    return pl.pallas_call(
        kernel,
        out_shape=jax.ShapeDtypeStruct((kept, batches * rows, width), jnp.bfloat16),
        in_specs=[vmem, pl.BlockSpec(memory_space=pl.ANY)] + [vmem] * 6,
        out_specs=vmem,
        scratch_shapes=[
            pltpu.VMEM((kept, places * shard, width), jnp.bfloat16),
            pltpu.VMEM((kept, batches, rows, width), jnp.float32),
            pltpu.VMEM((batches, edges, rows), jnp.bfloat16),
            pltpu.VMEM((batches, rows, width), jnp.bfloat16),
            pltpu.VMEM((kept, batches, edges, width), jnp.bfloat16),
            pltpu.VMEM((kept, batches, edges, width), jnp.bfloat16),
            dma((kept,)),
            dma((kept, places)),
            dma((kept, chips)),
            dma((kept, chips)),
            dma((kept, chips)),
            dma((kept, batches, len(OFFSETS))),
            dma((kept, batches, len(OFFSETS))),
            dma((batches,)),
            dma((batches,)),
        ],
        compiler_params=pltpu.CompilerParams(
            collective_id=0, has_side_effects=True, vmem_limit_bytes=40 * 1024 * 1024
        ),
    )(
        features,
        weights,
        history,
        own_adj,
        side_adj.reshape(batches, edges, rows),
        hist_adj,
        send_ids,
        hist_ids,
    )


def device_part(features, weights, *rest):
    places = lax.axis_size("graph")
    whole_tiles = weights.shape[1] % TILE_ROWS == 0 and rest[2].shape[2] % TILE_ROWS == 0
    if whole_tiles and places % 2 == 0 and weights.shape[0] % lax.axis_size("segment") == 0:
        return staged(features, weights, *rest)
    return shards(features, weights, *rest)


def solution(mesh):
    in_specs = (
        P("graph", None),
        P(None, "graph", None),
        P(None, "graph", None),
        P(None, "graph", None),
        P(None, None, "graph", None),
        P(None, "graph", None),
        P(None, None, "graph"),
        P(None, "graph"),
    )
    out_specs = P("segment", "graph", None)
    return jax.shard_map(device_part, mesh=mesh, in_specs=in_specs, out_specs=out_specs, check_vma=False)
```

```python
import math

import jax
import jax.numpy as jnp
from jax import lax
from jax.experimental import pallas as pl
from jax.experimental.pallas import tpu as pltpu
from jax.sharding import PartitionSpec as P

ALPHA = 0.1
LAMBDA = 1.5
OFFSETS = (1, -1, 2, -2)


def shifted(value, axis, steps):
    count = lax.axis_size(axis)
    initial, last = (max(0, -steps), min(count, count - steps))
    return lax.ppermute(value, axis, [(source, source + steps) for source in range(initial, last)])


def propagate(
    current, initial, layer_number, weight, tables, own_tile, side_tile, send_rows, past_rows
):
    edge_count = send_rows.shape[1]
    picked = jnp.take(current, send_rows.reshape(-1), axis=0)
    arrived = []
    for direction in range(len(OFFSETS)):
        outgoing = picked[direction * edge_count : (direction + 1) * edge_count]
        arrived.append(shifted(outgoing, "graph", OFFSETS[direction]))
    layer_table = lax.dynamic_index_in_dim(tables, layer_number, 0, keepdims=False)
    arrived.append(jnp.take(layer_table, past_rows, axis=0))
    gathered_rows = jnp.concatenate(arrived, axis=0)
    aggregate = jnp.dot(own_tile, current, preferred_element_type=jnp.float32)
    aggregate = aggregate + lax.dot_general(
        side_tile, gathered_rows, (((0,), (0,)), ((), ())), preferred_element_type=jnp.float32
    )
    support = (1.0 - ALPHA) * aggregate + ALPHA * initial.astype(jnp.float32)
    mixing = jnp.dot(support.astype(jnp.bfloat16), weight, preferred_element_type=jnp.float32)
    strength = jnp.log(LAMBDA / (layer_number.astype(jnp.float32) + 1.0) + 1.0)
    return jax.nn.relu((1.0 - strength) * support + strength * mixing).astype(jnp.bfloat16)


def batch_tiles(own_adj, side_adj, hist_adj, send_ids, hist_ids, batch_safe):
    batch_rows = own_adj.shape[2]
    side_edges = side_adj.shape[1] * side_adj.shape[2]
    own_tile = lax.dynamic_index_in_dim(own_adj, batch_safe, 0, keepdims=False)
    edge_tile = lax.dynamic_index_in_dim(side_adj, batch_safe, 0, keepdims=False).reshape(
        side_edges, batch_rows
    )
    past_tile = lax.dynamic_index_in_dim(hist_adj, batch_safe, 0, keepdims=False)
    side_tile = jnp.concatenate([edge_tile, past_tile], axis=0)
    send_rows = lax.dynamic_index_in_dim(send_ids, batch_safe, 0, keepdims=False)
    past_rows = lax.dynamic_index_in_dim(hist_ids, batch_safe, 0, keepdims=False)
    return (own_tile, side_tile, send_rows, past_rows)


def shards(features, weights, history, own_adj, side_adj, hist_adj, send_ids, hist_ids):
    segment_pos = lax.axis_index("segment")
    segment_count = lax.axis_size("segment")
    batch_count = own_adj.shape[0]
    batch_rows = own_adj.shape[2]
    layer_total = weights.shape[0]
    kept_slots = layer_total // segment_count
    initial = lax.dynamic_slice_in_dim(features, segment_pos * batch_rows, batch_rows, 0)
    own_tile, side_tile, send_rows, past_rows = batch_tiles(
        own_adj, side_adj, hist_adj, send_ids, hist_ids, segment_pos
    )
    current = initial
    produced = []
    for number in range(layer_total):
        weight = lax.all_gather(weights[number], "graph", axis=0, tiled=True)
        current = propagate(
            current,
            initial,
            jnp.int32(number),
            weight,
            history,
            own_tile,
            side_tile,
            send_rows,
            past_rows,
        )
        produced.append(current)
    arranged = jnp.stack(
        [
            jnp.stack([produced[kept_slots * target + slot] for target in range(segment_count)])
            for slot in range(kept_slots)
        ]
    )
    received = lax.all_to_all(arranged, "segment", split_axis=1, concat_axis=1, tiled=True)
    return received.reshape(kept_slots, batch_count * batch_rows, features.shape[1])


TILE_ROWS = 16
MESH = pl.DeviceIdType.MESH


def column_of(row):
    count = row.shape[1]
    down = lax.broadcasted_iota(jnp.int32, (count, count), 0)
    across = lax.broadcasted_iota(jnp.int32, (count, count), 1)
    spread = jnp.broadcast_to(row.astype(jnp.float32), (count, count))
    return jnp.sum(jnp.where(down == across, spread, 0.0), axis=1, keepdims=True)


def selector(row, width):
    across = lax.broadcasted_iota(jnp.int32, (row.shape[1], width), 1).astype(jnp.float32)
    return jnp.where(across == column_of(row), 1.0, 0.0).astype(jnp.bfloat16)


def transposed_dot(left, right):
    return lax.dot_general(
        left, right, (((0,), (0,)), ((), ())), preferred_element_type=jnp.float32
    )


def stage_kernel(
    segments, places, layer_total,
    features_in, weights, history_in, own_in, side_in, hist_in, send_in, ids_in,
    out,
    features, history, own_adj, side_adj, hist_adj, send_ids, hist_ids,
    made, full, base, select, entering, leaving, arrived,
    load_sem, own_sem, store_sem, line_recv, mate_recv, pair_recv, shard_recv,
    up_send, down_send, mate_send, pair_send, shard_send,
    edge_send, edge_recv, hop_send, hop_recv,
):
    seg = lax.axis_index("segment")
    me = lax.axis_index("graph")
    kept = layer_total // segments
    batches, rows = own_adj.shape[0], own_adj.shape[2]
    shard = weights.shape[1]
    piece = shard // 2
    edge = send_ids.shape[2]
    chips = places // 2
    chip = me // 2
    core = me % 2
    pair = me + 1 - 2 * core
    half = segments // 2
    side = seg // half
    mate = seg + half - 2 * half * side
    first_layer = seg * kept

    loads = [
        pltpu.make_async_copy(source, target, load_sem.at[number])
        for number, (source, target) in enumerate(
            [
                (features_in, features),
                (history_in.at[pl.ds(first_layer, kept)], history),
                (own_in, own_adj),
                (side_in, side_adj),
                (hist_in, hist_adj),
                (send_in, send_ids),
                (ids_in, hist_ids),
            ]
        )
    ]
    for load in loads:
        load.start()

    barrier = pltpu.get_barrier_semaphore()
    expected = jnp.int32(1)
    pl.semaphore_signal(barrier, inc=1, device_id={"segment": mate}, device_id_type=MESH)
    for offset in OFFSETS:
        there = me + offset
        inside = jnp.logical_and(there >= 0, there < places)

        @pl.when(inside)
        def _():
            pl.semaphore_signal(barrier, inc=1, device_id={"graph": there}, device_id_type=MESH)

        expected = expected + inside.astype(jnp.int32)
    for step in (1, -1):
        beside = seg + step
        inside = jnp.logical_and(beside >= 0, beside < segments)

        @pl.when(inside)
        def _():
            pl.semaphore_signal(
                barrier, inc=1, device_id={"segment": beside}, device_id_type=MESH
            )

        expected = expected + inside.astype(jnp.int32)
    pl.semaphore_wait(barrier, expected)


    def shard_rows(owner):
        return pl.ds(pl.multiple_of(owner * shard, shard), shard)

    def piece_rows(owner, which):
        return pl.ds(pl.multiple_of(owner * shard + which * piece, piece), piece)

    def whole_shard(slot):
        return weights.at[first_layer + slot]

    def own_copy(slot):
        return pltpu.make_async_copy(
            whole_shard(slot), full.at[side, slot, shard_rows(me)], own_sem.at[slot]
        )

    def push(turn, slot, source, owner, which, target, send_sem, recv_sem):
        return pltpu.make_async_remote_copy(
            src_ref=source,
            dst_ref=full.at[turn, slot, piece_rows(owner, which)],
            send_sem=send_sem,
            recv_sem=recv_sem,
            device_id=target,
            device_id_type=MESH,
        )

    def held(turn, slot, owner, which):
        return full.at[turn, slot, piece_rows(owner, which)]

    def along(turn, slot, source, owner, step, send_sem):
        return push(
            turn, slot, source, owner, side, {"graph": me + 2 * step},
            send_sem.at[turn, slot, owner // 2], line_recv.at[turn, slot, owner // 2],
        )

    def to_pair(slot, owner, which):
        return push(
            side, slot, held(side, slot, owner, which), owner, which, {"graph": pair},
            pair_send.at[slot, which, owner // 2], pair_recv.at[slot, which, owner // 2],
        )

    def to_mate(slot, owner):
        turn = 1 - side
        return push(
            turn, slot, held(turn, slot, owner, side), owner, side, {"segment": mate},
            mate_send.at[slot, owner // 2], mate_recv.at[slot, owner // 2],
        )

    def from_mate(slot, owner):
        which = 1 - side
        return push(
            side, slot, held(side, slot, owner, which), owner, which, {"segment": mate},
            mate_send.at[slot, owner // 2], mate_recv.at[slot, owner // 2],
        )

    def shard_to_pair(slot, source, owner):
        return pltpu.make_async_remote_copy(
            src_ref=source,
            dst_ref=full.at[side, slot, shard_rows(owner)],
            send_sem=shard_send.at[slot],
            recv_sem=shard_recv.at[slot],
            device_id={"graph": pair},
            device_id_type=MESH,
        )

    def open_slot(turn, slot):
        number = (seg + (turn - side) * half) * kept + slot
        source = weights.at[number, pl.ds(pl.multiple_of(side * piece, piece), piece)]

        @pl.when(chip < chips - 1)
        def _():
            along(turn, slot, source, me, 1, up_send).start()

        @pl.when(chip > 0)
        def _():
            along(turn, slot, source, me, -1, down_send).start()

        @pl.when(side == turn)
        def _():
            shard_to_pair(slot, whole_shard(slot), me).start()
            own_copy(slot).start()

    def hand_on(turn, slot, owner):
        @pl.when(side == turn)
        def _():
            to_pair(slot, owner, side).start()

        @pl.when(side != turn)
        def _():
            to_mate(slot, owner).start()

    def relay(turn, slot, distance):
        below = me - 2 * distance

        @pl.when(below >= 0)
        def _():
            block = held(turn, slot, below, side)
            along(turn, slot, block, below, 1, up_send).wait_recv()

            @pl.when(chip < chips - 1)
            def _():
                along(turn, slot, block, below, 1, up_send).start()

            hand_on(turn, slot, below)

        above = me + 2 * distance

        @pl.when(above < places)
        def _():
            block = held(turn, slot, above, side)
            along(turn, slot, block, above, -1, down_send).wait_recv()

            @pl.when(chip > 0)
            def _():
                along(turn, slot, block, above, -1, down_send).start()

            hand_on(turn, slot, above)

    def bridge(slot, distance):
        for owner in (me - 2 * distance, me + 2 * distance):

            @pl.when(jnp.logical_and(owner >= 0, owner < places))
            def _():
                from_mate(slot, owner).wait_recv()
                to_pair(slot, owner, 1 - side).start()

    def close_slot(slot):
        own_copy(slot).wait()
        shard_to_pair(slot, full.at[side, slot, shard_rows(pair)], pair).wait_recv()

        def from_pair(other, carry):
            @pl.when(other != chip)
            def _():
                owner = 2 * other + 1 - core
                for which in range(2):
                    to_pair(slot, owner, which).wait_recv()

            return carry

        lax.fori_loop(0, chips, from_pair, 0)

    def edge_copy(slot, batch, direction):
        part = pl.ds(direction * edge, edge)
        return pltpu.make_async_remote_copy(
            src_ref=leaving.at[slot, batch, part],
            dst_ref=arrived.at[slot, batch, part],
            send_sem=edge_send.at[slot, batch, direction],
            recv_sem=edge_recv.at[slot, batch, direction],
            device_id={"graph": me + OFFSETS[direction]},
            device_id_type=MESH,
        )

    def sends(direction):
        there = me + OFFSETS[direction]
        return jnp.logical_and(there >= 0, there < places)

    def receives(direction):
        there = me - OFFSETS[direction]
        return jnp.logical_and(there >= 0, there < places)

    def send_edges(slot, batch, current):
        leaving[slot, batch] = jnp.dot(
            select[batch], current, preferred_element_type=jnp.float32
        ).astype(jnp.bfloat16)
        for direction in range(len(OFFSETS)):

            @pl.when(sends(direction))
            def _():
                edge_copy(slot, batch, direction).start()

    def batch_range(batch):
        return pl.ds(pl.multiple_of(batch * rows, rows), rows)

    def store(slot, batch):
        return pltpu.make_async_copy(
            made.at[slot, batch_range(batch)],
            out.at[slot, batch_range(batch)],
            store_sem.at[slot, batch],
        )

    def hop(batch):
        return pltpu.make_async_remote_copy(
            src_ref=made.at[kept - 1, batch_range(batch)],
            dst_ref=entering.at[batch],
            send_sem=hop_send.at[batch],
            recv_sem=hop_recv.at[batch],
            device_id={"segment": seg + 1},
            device_id_type=MESH,
        )

    def prepare(batch, carry):
        for direction in range(len(OFFSETS)):
            part = pl.ds(direction * edge, edge)
            select[batch, part] = selector(
                send_ids[batch, pl.ds(direction, 1), :], rows
            )
            for slot in range(kept):

                @pl.when(jnp.logical_not(receives(direction)))
                def _():
                    arrived[slot, batch, part] = jnp.zeros(
                        (edge, arrived.shape[3]), jnp.bfloat16
                    )

        initial = features[batch_range(batch), :]

        @pl.when(seg == 0)
        def _():
            entering[batch] = initial

        lookup = selector(hist_ids[pl.ds(batch, 1), :], history.shape[1])
        for slot in range(kept):
            looked = jnp.dot(
                lookup, history[slot], preferred_element_type=jnp.float32
            ).astype(jnp.bfloat16)
            past = transposed_dot(hist_adj[batch], looked)
            base[slot, batch] = (1.0 - ALPHA) * past + ALPHA * initial.astype(jnp.float32)
        return carry

    def layer(slot, batch):
        strength = jnp.float32(0.0)
        for number in range(layer_total):
            value = math.log(LAMBDA / (number + 1.0) + 1.0)
            strength = jnp.where(first_layer + slot == number, jnp.float32(value), strength)
        if slot == 0:
            current = entering[batch]
        else:
            current = made[slot - 1, batch_range(batch), :]
        aggregate = jnp.dot(own_adj[batch], current, preferred_element_type=jnp.float32)
        for direction in range(len(OFFSETS)):

            @pl.when(receives(direction))
            def _():
                edge_copy(slot, batch, direction).wait_recv()

        aggregate = aggregate + transposed_dot(side_adj[batch], arrived[slot, batch])
        support = (1.0 - ALPHA) * aggregate + base[slot, batch]
        mixing = jnp.dot(
            support.astype(jnp.bfloat16), full[side, slot], preferred_element_type=jnp.float32
        )
        result = jnp.maximum((1.0 - strength) * support + strength * mixing, 0.0)
        result = result.astype(jnp.bfloat16)
        made[slot, batch_range(batch), :] = result
        store(slot, batch).start()
        if slot < kept - 1:
            send_edges(slot + 1, batch, result)
        else:

            @pl.when(seg < segments - 1)
            def _():
                hop(batch).start()

    far = chips - 1

    def line_steps(turn, slot):
        steps = []
        for distance in range(1, chips):
            work = [(relay, (turn, slot, distance))]
            if distance == max(1, far - 1):
                if slot < kept - 1:
                    work.append((open_slot, (turn, slot + 1)))
                elif turn == 0:
                    work.append((open_slot, (1, 0)))
            steps.append(work)
        return steps

    def run(work):
        for action, arguments in work:
            action(*arguments)

    def bridges(slot):
        for distance in range(1, chips):
            bridge(slot, distance)

    open_slot(0, 0)
    for load in loads:
        load.wait()
    lax.fori_loop(0, batches, prepare, 0)
    for work in line_steps(0, 0):
        run(work)

    @pl.when(side == 0)
    def _():
        bridges(0)

    last_first = batches * kept - 1
    last_other = batches + kept - 2
    first_tasks = [[] for _ in range(last_first + 1)]
    other_tasks = [[] for _ in range(last_other + 1)]
    later = []
    for slot in range(1, kept):
        steps = line_steps(0, slot)
        for distance in range(1, chips):
            if distance > 1:
                steps[distance - 1].append((bridge, (slot, distance - 1)))
        steps.append([(bridge, (slot, far))])
        for number, work in enumerate(steps):
            first_tasks[min((slot - 1) * batches + number, slot * batches - 1)] += work
        later += steps
    shared = []
    for slot in range(kept):
        shared += line_steps(1, slot)
    for number, work in enumerate(shared):
        first_tasks[min((kept - 1) * batches + number, last_first)] += work
    for number, work in enumerate(shared[far:]):
        other_tasks[min(number, last_other)] += work

    @pl.when(jnp.logical_and(seg > 0, side == 0))
    def _():
        for work in later + shared[:far]:
            run(work)

    @pl.when(side == 1)
    def _():
        for slot in range(1, kept):
            for work in line_steps(0, slot):
                run(work)
        for work in shared:
            run(work)
        for slot in range(kept):
            bridges(slot)

    lag = jnp.where(seg == 0, batches, 1)
    ticks = batches + lag * (kept - 1)

    def tick(time, carry):
        @pl.when(time < batches)
        def _():
            @pl.when(seg > 0)
            def _():
                hop(time).wait_recv()

            send_edges(0, time, entering[time])

        for number, work in enumerate(first_tasks):

            @pl.when(jnp.logical_and(seg == 0, time == number))
            def _():
                run(work)

        for slot in range(kept - 1, -1, -1):

            @pl.when(time == lag * slot)
            def _():
                close_slot(slot)

            batch = time - lag * slot

            @pl.when(jnp.logical_and(batch >= 0, batch < batches))
            def _():
                layer(slot, batch)

        for number, work in enumerate(other_tasks):

            @pl.when(jnp.logical_and(jnp.logical_and(seg > 0, side == 0), time == number))
            def _():
                run(work)

        return carry

    lax.fori_loop(0, ticks, tick, 0)

    def finish(batch, carry):
        for slot in range(kept):
            store(slot, batch).wait()
            for direction in range(len(OFFSETS)):

                @pl.when(sends(direction))
                def _():
                    edge_copy(slot, batch, direction).wait_send()

        @pl.when(seg < segments - 1)
        def _():
            hop(batch).wait_send()

        return carry

    lax.fori_loop(0, batches, finish, 0)

    def drain(other, carry):
        owner = 2 * other + core
        for slot in range(kept):
            for turn in range(2):
                block = held(turn, slot, owner, side)

                @pl.when(jnp.logical_and(other <= chip, chip < chips - 1))
                def _():
                    along(turn, slot, block, owner, 1, up_send).wait_send()

                @pl.when(jnp.logical_and(other >= chip, chip > 0))
                def _():
                    along(turn, slot, block, owner, -1, down_send).wait_send()

            @pl.when(other != chip)
            def _():
                to_mate(slot, owner).wait_send()
                for which in range(2):
                    to_pair(slot, owner, which).wait_send()

            @pl.when(other == chip)
            def _():
                shard_to_pair(slot, whole_shard(slot), owner).wait_send()

        return carry

    lax.fori_loop(0, chips, drain, 0)


def staged(features, weights, history, own_adj, side_adj, hist_adj, send_ids, hist_ids):
    segments = lax.axis_size("segment")
    places = lax.axis_size("graph")
    layer_total, shard, width = weights.shape
    kept = layer_total // segments
    batches, rows = own_adj.shape[0], own_adj.shape[2]
    edges = side_adj.shape[1] * side_adj.shape[2]
    chips = places // 2
    dma = pltpu.SemaphoreType.DMA

    def kernel(*refs):
        stage_kernel(segments, places, layer_total, *refs)

    anywhere = pl.BlockSpec(memory_space=pl.ANY)
    half = jnp.bfloat16
    return pl.pallas_call(
        kernel,
        out_shape=jax.ShapeDtypeStruct((kept, batches * rows, width), half),
        in_specs=[anywhere] * 8,
        out_specs=anywhere,
        scratch_shapes=[
            pltpu.VMEM(features.shape, half),
            pltpu.VMEM((kept,) + history.shape[1:], half),
            pltpu.VMEM(own_adj.shape, half),
            pltpu.VMEM((batches, edges, rows), half),
            pltpu.VMEM(hist_adj.shape, half),
            pltpu.VMEM(send_ids.shape, send_ids.dtype),
            pltpu.VMEM(hist_ids.shape, hist_ids.dtype),
            pltpu.VMEM((kept, batches * rows, width), half),
            pltpu.VMEM((2, kept, places * shard, width), half),
            pltpu.VMEM((kept, batches, rows, width), jnp.float32),
            pltpu.VMEM((batches, edges, rows), half),
            pltpu.VMEM((batches, rows, width), half),
            pltpu.VMEM((kept, batches, edges, width), half),
            pltpu.VMEM((kept, batches, edges, width), half),
            dma((7,)),
            dma((kept,)),
            dma((kept, batches)),
            dma((2, kept, chips)),
            dma((kept, chips)),
            dma((kept, 2, chips)),
            dma((kept,)),
            dma((2, kept, chips)),
            dma((2, kept, chips)),
            dma((kept, chips)),
            dma((kept, 2, chips)),
            dma((kept,)),
            dma((kept, batches, len(OFFSETS))),
            dma((kept, batches, len(OFFSETS))),
            dma((batches,)),
            dma((batches,)),
        ],
        compiler_params=pltpu.CompilerParams(
            collective_id=0, has_side_effects=True, vmem_limit_bytes=60 * 1024 * 1024
        ),
    )(
        features,
        weights,
        history,
        own_adj,
        side_adj.reshape(batches, edges, rows),
        hist_adj,
        send_ids,
        hist_ids,
    )


def device_part(features, weights, *rest):
    places, segments = lax.axis_size("graph"), lax.axis_size("segment")
    whole_tiles = weights.shape[1] % (2 * TILE_ROWS) == 0 and rest[2].shape[2] % TILE_ROWS == 0
    even = places % 2 == 0 and segments % 2 == 0 and weights.shape[0] % segments == 0
    if whole_tiles and even:
        return staged(features, weights, *rest)
    return shards(features, weights, *rest)


def solution(mesh):
    in_specs = (
        P("graph", None),
        P(None, "graph", None),
        P(None, "graph", None),
        P(None, "graph", None),
        P(None, None, "graph", None),
        P(None, "graph", None),
        P(None, None, "graph"),
        P(None, "graph"),
    )
    out_specs = P("segment", "graph", None)
    return jax.shard_map(device_part, mesh=mesh, in_specs=in_specs, out_specs=out_specs, check_vma=False)
```

```python
import math

import jax
import jax.numpy as jnp
from jax import lax
from jax.experimental import pallas as pl
from jax.experimental.pallas import tpu as pltpu
from jax.sharding import PartitionSpec as P

ALPHA = 0.1
LAMBDA = 1.5
OFFSETS = (1, -1, 2, -2)


def shifted(value, axis, steps):
    count = lax.axis_size(axis)
    initial, last = (max(0, -steps), min(count, count - steps))
    return lax.ppermute(value, axis, [(source, source + steps) for source in range(initial, last)])


def propagate(
    current, initial, layer_number, weight, tables, own_tile, side_tile, send_rows, past_rows
):
    edge_count = send_rows.shape[1]
    picked = jnp.take(current, send_rows.reshape(-1), axis=0)
    arrived = []
    for direction in range(len(OFFSETS)):
        outgoing = picked[direction * edge_count : (direction + 1) * edge_count]
        arrived.append(shifted(outgoing, "graph", OFFSETS[direction]))
    layer_table = lax.dynamic_index_in_dim(tables, layer_number, 0, keepdims=False)
    arrived.append(jnp.take(layer_table, past_rows, axis=0))
    gathered_rows = jnp.concatenate(arrived, axis=0)
    aggregate = jnp.dot(own_tile, current, preferred_element_type=jnp.float32)
    aggregate = aggregate + lax.dot_general(
        side_tile, gathered_rows, (((0,), (0,)), ((), ())), preferred_element_type=jnp.float32
    )
    support = (1.0 - ALPHA) * aggregate + ALPHA * initial.astype(jnp.float32)
    mixing = jnp.dot(support.astype(jnp.bfloat16), weight, preferred_element_type=jnp.float32)
    strength = jnp.log(LAMBDA / (layer_number.astype(jnp.float32) + 1.0) + 1.0)
    return jax.nn.relu((1.0 - strength) * support + strength * mixing).astype(jnp.bfloat16)


def batch_tiles(own_adj, side_adj, hist_adj, send_ids, hist_ids, batch_safe):
    batch_rows = own_adj.shape[2]
    side_edges = side_adj.shape[1] * side_adj.shape[2]
    own_tile = lax.dynamic_index_in_dim(own_adj, batch_safe, 0, keepdims=False)
    edge_tile = lax.dynamic_index_in_dim(side_adj, batch_safe, 0, keepdims=False).reshape(
        side_edges, batch_rows
    )
    past_tile = lax.dynamic_index_in_dim(hist_adj, batch_safe, 0, keepdims=False)
    side_tile = jnp.concatenate([edge_tile, past_tile], axis=0)
    send_rows = lax.dynamic_index_in_dim(send_ids, batch_safe, 0, keepdims=False)
    past_rows = lax.dynamic_index_in_dim(hist_ids, batch_safe, 0, keepdims=False)
    return (own_tile, side_tile, send_rows, past_rows)


def shards(features, weights, history, own_adj, side_adj, hist_adj, send_ids, hist_ids):
    segment_pos = lax.axis_index("segment")
    segment_count = lax.axis_size("segment")
    batch_count = own_adj.shape[0]
    batch_rows = own_adj.shape[2]
    layer_total = weights.shape[0]
    kept_slots = layer_total // segment_count
    initial = lax.dynamic_slice_in_dim(features, segment_pos * batch_rows, batch_rows, 0)
    own_tile, side_tile, send_rows, past_rows = batch_tiles(
        own_adj, side_adj, hist_adj, send_ids, hist_ids, segment_pos
    )
    current = initial
    produced = []
    for number in range(layer_total):
        weight = lax.all_gather(weights[number], "graph", axis=0, tiled=True)
        current = propagate(
            current,
            initial,
            jnp.int32(number),
            weight,
            history,
            own_tile,
            side_tile,
            send_rows,
            past_rows,
        )
        produced.append(current)
    arranged = jnp.stack(
        [
            jnp.stack([produced[kept_slots * target + slot] for target in range(segment_count)])
            for slot in range(kept_slots)
        ]
    )
    received = lax.all_to_all(arranged, "segment", split_axis=1, concat_axis=1, tiled=True)
    return received.reshape(kept_slots, batch_count * batch_rows, features.shape[1])


TILE_ROWS = 16
MESH = pl.DeviceIdType.MESH


def column_of(row):
    count = row.shape[1]
    down = lax.broadcasted_iota(jnp.int32, (count, count), 0)
    across = lax.broadcasted_iota(jnp.int32, (count, count), 1)
    spread = jnp.broadcast_to(row.astype(jnp.float32), (count, count))
    return jnp.sum(jnp.where(down == across, spread, 0.0), axis=1, keepdims=True)


def selector(row, width):
    across = lax.broadcasted_iota(jnp.int32, (row.shape[1], width), 1).astype(jnp.float32)
    return jnp.where(across == column_of(row), 1.0, 0.0).astype(jnp.bfloat16)


def transposed_dot(left, right):
    return lax.dot_general(
        left, right, (((0,), (0,)), ((), ())), preferred_element_type=jnp.float32
    )


def stage_kernel(
    segments, places, layer_total,
    features_in, weights, history_in, own_in, side_in, hist_in, send_in, ids_in,
    out,
    features, history, own_adj, side_adj, hist_adj, send_ids, hist_ids,
    full, base, select, entering, leaving, arrived,
    load_sem, own_sem, line_recv, mate_recv, pair_recv, shard_recv,
    up_send, down_send, line_send, mate_send, pair_send, shard_send,
    edge_send, edge_recv, hop_send, hop_recv,
):
    seg = lax.axis_index("segment")
    me = lax.axis_index("graph")
    kept = layer_total // segments
    batches, rows = own_adj.shape[0], own_adj.shape[2]
    shard = weights.shape[1]
    piece = shard // 2
    edge = send_ids.shape[2]
    chips = places // 2
    chip = me // 2
    core = me % 2
    pair = me + 1 - 2 * core
    half = segments // 2
    side = seg // half
    mate = seg + half - 2 * half * side
    first_layer = seg * kept

    loads = [
        pltpu.make_async_copy(source, target, load_sem.at[number])
        for number, (source, target) in enumerate(
            [
                (features_in, features),
                (history_in.at[pl.ds(first_layer, kept)], history),
                (own_in, own_adj),
                (side_in, side_adj),
                (hist_in, hist_adj),
                (send_in, send_ids),
                (ids_in, hist_ids),
            ]
        )
    ]
    for load in loads:
        load.start()

    barrier = pltpu.get_barrier_semaphore()
    expected = jnp.int32(1)
    pl.semaphore_signal(barrier, inc=1, device_id={"segment": mate}, device_id_type=MESH)
    for offset in OFFSETS:
        there = me + offset
        inside = jnp.logical_and(there >= 0, there < places)

        @pl.when(inside)
        def _():
            pl.semaphore_signal(barrier, inc=1, device_id={"graph": there}, device_id_type=MESH)

        expected = expected + inside.astype(jnp.int32)
    for step in (1, -1):
        beside = seg + step
        inside = jnp.logical_and(beside >= 0, beside < segments)

        @pl.when(inside)
        def _():
            pl.semaphore_signal(
                barrier, inc=1, device_id={"segment": beside}, device_id_type=MESH
            )

        expected = expected + inside.astype(jnp.int32)
    pl.semaphore_wait(barrier, expected)


    def shard_rows(owner):
        return pl.ds(pl.multiple_of(owner * shard, shard), shard)

    def piece_rows(owner, which):
        return pl.ds(pl.multiple_of(owner * shard + which * piece, piece), piece)

    def whole_shard(slot):
        return weights.at[first_layer + slot]

    def own_copy(slot):
        return pltpu.make_async_copy(
            whole_shard(slot), full.at[side, slot, shard_rows(me)], own_sem.at[slot]
        )

    def push(turn, slot, source, owner, which, target, send_sem, recv_sem):
        return pltpu.make_async_remote_copy(
            src_ref=source,
            dst_ref=full.at[turn, slot, piece_rows(owner, which)],
            send_sem=send_sem,
            recv_sem=recv_sem,
            device_id=target,
            device_id_type=MESH,
        )

    def held(turn, slot, owner, which):
        return full.at[turn, slot, piece_rows(owner, which)]

    def along(slot, source, owner, step, send_sem):
        return push(
            0, slot, source, owner, side, {"graph": me + 2 * step},
            send_sem.at[slot, owner // 2], line_recv.at[0, slot, owner // 2],
        )

    def direct(slot, source, owner, target):
        return push(
            1, slot, source, owner, side, {"graph": target},
            line_send.at[slot, target // 2], line_recv.at[1, slot, owner // 2],
        )

    def to_pair(slot, owner, which):
        return push(
            side, slot, held(side, slot, owner, which), owner, which, {"graph": pair},
            pair_send.at[slot, which, owner // 2], pair_recv.at[slot, which, owner // 2],
        )

    def to_mate(slot, owner):
        turn = 1 - side
        return push(
            turn, slot, held(turn, slot, owner, side), owner, side, {"segment": mate},
            mate_send.at[slot, owner // 2], mate_recv.at[slot, owner // 2],
        )

    def from_mate(slot, owner):
        which = 1 - side
        return push(
            side, slot, held(side, slot, owner, which), owner, which, {"segment": mate},
            mate_send.at[slot, owner // 2], mate_recv.at[slot, owner // 2],
        )

    def shard_to_pair(slot, source, owner):
        return pltpu.make_async_remote_copy(
            src_ref=source,
            dst_ref=full.at[side, slot, shard_rows(owner)],
            send_sem=shard_send.at[slot],
            recv_sem=shard_recv.at[slot],
            device_id={"graph": pair},
            device_id_type=MESH,
        )

    def half_shard(turn, slot):
        number = (seg + (turn - side) * half) * kept + slot
        return weights.at[number, pl.ds(pl.multiple_of(side * piece, piece), piece)]

    def place_own(turn, slot):
        @pl.when(side == turn)
        def _():
            shard_to_pair(slot, whole_shard(slot), me).start()
            own_copy(slot).start()

    def open_slot(slot):
        source = half_shard(0, slot)

        @pl.when(chip < chips - 1)
        def _():
            along(slot, source, me, 1, up_send).start()

        @pl.when(chip > 0)
        def _():
            along(slot, source, me, -1, down_send).start()

        place_own(0, slot)

    def around(distance, action):
        for owner in (me - 2 * distance, me + 2 * distance):

            @pl.when(jnp.logical_and(owner >= 0, owner < places))
            def _():
                action(owner)

    def open_second(slot):
        source = half_shard(1, slot)
        for distance in range(1, chips):
            around(distance, lambda target: direct(slot, source, me, target).start())
        place_own(1, slot)

    def hand_on(turn, slot, owner):
        @pl.when(side == turn)
        def _():
            to_pair(slot, owner, side).start()

        @pl.when(side != turn)
        def _():
            to_mate(slot, owner).start()

    def relay(slot, distance):
        below = me - 2 * distance

        @pl.when(below >= 0)
        def _():
            block = held(0, slot, below, side)
            along(slot, block, below, 1, up_send).wait_recv()

            @pl.when(chip < chips - 1)
            def _():
                along(slot, block, below, 1, up_send).start()

            hand_on(0, slot, below)

        above = me + 2 * distance

        @pl.when(above < places)
        def _():
            block = held(0, slot, above, side)
            along(slot, block, above, -1, down_send).wait_recv()

            @pl.when(chip > 0)
            def _():
                along(slot, block, above, -1, down_send).start()

            hand_on(0, slot, above)

    def hand_second(slot):
        def one(owner):
            direct(slot, held(1, slot, owner, side), owner, owner).wait_recv()
            hand_on(1, slot, owner)

        for distance in range(1, chips):
            around(distance, one)

    def bridge(slot, distance):
        for owner in (me - 2 * distance, me + 2 * distance):

            @pl.when(jnp.logical_and(owner >= 0, owner < places))
            def _():
                from_mate(slot, owner).wait_recv()
                to_pair(slot, owner, 1 - side).start()

    def close_slot(slot):
        own_copy(slot).wait()
        shard_to_pair(slot, full.at[side, slot, shard_rows(pair)], pair).wait_recv()

        def from_pair(other, carry):
            @pl.when(other != chip)
            def _():
                owner = 2 * other + 1 - core
                for which in range(2):
                    to_pair(slot, owner, which).wait_recv()

            return carry

        lax.fori_loop(0, chips, from_pair, 0)

    def edge_copy(slot, batch, direction):
        part = pl.ds(direction * edge, edge)
        return pltpu.make_async_remote_copy(
            src_ref=leaving.at[slot, batch, part],
            dst_ref=arrived.at[slot, batch, part],
            send_sem=edge_send.at[slot, batch, direction],
            recv_sem=edge_recv.at[slot, batch, direction],
            device_id={"graph": me + OFFSETS[direction]},
            device_id_type=MESH,
        )

    def sends(direction):
        there = me + OFFSETS[direction]
        return jnp.logical_and(there >= 0, there < places)

    def receives(direction):
        there = me - OFFSETS[direction]
        return jnp.logical_and(there >= 0, there < places)

    def send_edges(slot, batch, current):
        leaving[slot, batch] = jnp.dot(
            select[batch], current, preferred_element_type=jnp.float32
        ).astype(jnp.bfloat16)
        for direction in range(len(OFFSETS)):

            @pl.when(sends(direction))
            def _():
                edge_copy(slot, batch, direction).start()

    def batch_range(batch):
        return pl.ds(pl.multiple_of(batch * rows, rows), rows)

    def hop(batch):
        return pltpu.make_async_remote_copy(
            src_ref=out.at[kept - 1, batch_range(batch)],
            dst_ref=entering.at[batch],
            send_sem=hop_send.at[batch],
            recv_sem=hop_recv.at[batch],
            device_id={"segment": seg + 1},
            device_id_type=MESH,
        )

    def prepare(batch, carry):
        for direction in range(len(OFFSETS)):
            part = pl.ds(direction * edge, edge)
            select[batch, part] = selector(
                send_ids[batch, pl.ds(direction, 1), :], rows
            )
            for slot in range(kept):

                @pl.when(jnp.logical_not(receives(direction)))
                def _():
                    arrived[slot, batch, part] = jnp.zeros(
                        (edge, arrived.shape[3]), jnp.bfloat16
                    )

        initial = features[batch_range(batch), :]

        @pl.when(seg == 0)
        def _():
            entering[batch] = initial

        lookup = selector(hist_ids[pl.ds(batch, 1), :], history.shape[1])
        for slot in range(kept):
            looked = jnp.dot(
                lookup, history[slot], preferred_element_type=jnp.float32
            ).astype(jnp.bfloat16)
            past = transposed_dot(hist_adj[batch], looked)
            base[slot, batch] = (1.0 - ALPHA) * past + ALPHA * initial.astype(jnp.float32)
        return carry

    def layer(slot, batch):
        strength = jnp.float32(0.0)
        for number in range(layer_total):
            value = math.log(LAMBDA / (number + 1.0) + 1.0)
            strength = jnp.where(first_layer + slot == number, jnp.float32(value), strength)
        if slot == 0:
            current = entering[batch]
        else:
            current = out[slot - 1, batch_range(batch), :]
        aggregate = jnp.dot(own_adj[batch], current, preferred_element_type=jnp.float32)
        for direction in range(len(OFFSETS)):

            @pl.when(receives(direction))
            def _():
                edge_copy(slot, batch, direction).wait_recv()

        aggregate = aggregate + transposed_dot(side_adj[batch], arrived[slot, batch])
        support = (1.0 - ALPHA) * aggregate + base[slot, batch]
        mixing = jnp.dot(
            support.astype(jnp.bfloat16), full[side, slot], preferred_element_type=jnp.float32
        )
        result = jnp.maximum((1.0 - strength) * support + strength * mixing, 0.0)
        result = result.astype(jnp.bfloat16)
        out[slot, batch_range(batch), :] = result
        if slot < kept - 1:
            send_edges(slot + 1, batch, result)
        else:

            @pl.when(seg < segments - 1)
            def _():
                hop(batch).start()

    far = chips - 1

    def bridges(slot):
        for distance in range(1, chips):
            bridge(slot, distance)

    def line_steps(slot):
        steps = []
        for distance in range(1, chips):
            work = [(relay, (slot, distance))]
            if distance == max(1, far - 1) and slot < kept - 1:
                work.append((open_slot, (slot + 1,)))
            if distance == far and slot == kept - 1:
                work += [(open_second, (number,)) for number in range(kept)]
            if distance > 1:
                work.append((bridge, (slot, distance - 1)))
            steps.append(work)
        steps.append([(bridge, (slot, far))])
        return steps

    def run(work, bridging):
        for action, arguments in work:
            if action is not bridge:
                action(*arguments)
            elif bridging:

                @pl.when(side == 0)
                def _():
                    action(*arguments)

    open_slot(0)
    for load in loads:
        load.wait()
    middle = batches // 2
    lax.fori_loop(0, middle, prepare, 0)
    for number, work in enumerate(line_steps(0)):
        run(work, True)
        if number == 0:
            lax.fori_loop(middle, batches, prepare, 0)

            @pl.when(seg == 0)
            def _():
                def early(batch, carry):
                    send_edges(0, batch, entering[batch])
                    return carry

                lax.fori_loop(0, batches, early, 0)

    first_tasks = [[] for _ in range(batches * kept)]
    for slot in range(1, kept):
        for number, work in enumerate(line_steps(slot)):
            first_tasks[min((slot - 1) * batches + number, slot * batches - 1)] += work

    @pl.when(seg > 0)
    def _():
        for slot in range(1, kept):
            for work in line_steps(slot):
                run(work, True)

    @pl.when(side == 1)
    def _():
        for slot in range(kept):
            hand_second(slot)
        for slot in range(kept):
            bridges(slot)

    lag = jnp.where(seg == 0, batches, 1)
    ticks = batches + lag * (kept - 1)

    def tick(time, carry):
        @pl.when(jnp.logical_and(seg > 0, time < batches))
        def _():
            hop(time).wait_recv()
            send_edges(0, time, entering[time])

        for number, work in enumerate(first_tasks):
            if work:

                @pl.when(jnp.logical_and(seg == 0, time == number))
                def _():
                    run(work, True)

        for slot in range(kept - 1, -1, -1):

            @pl.when(time == lag * slot)
            def _():
                close_slot(slot)

            batch = time - lag * slot

            @pl.when(jnp.logical_and(batch >= 0, batch < batches))
            def _():
                layer(slot, batch)

        for slot in range(kept):

            @pl.when(
                jnp.logical_and(
                    jnp.logical_and(seg > 0, side == 0),
                    time == min(2 * slot + 1, batches + kept - 2),
                )
            )
            def _():
                hand_second(slot)

        return carry

    lax.fori_loop(0, ticks, tick, 0)

    @pl.when(seg == 0)
    def _():
        for slot in range(kept):
            hand_second(slot)

    def finish(batch, carry):
        for slot in range(kept):
            for direction in range(len(OFFSETS)):

                @pl.when(sends(direction))
                def _():
                    edge_copy(slot, batch, direction).wait_send()

        @pl.when(seg < segments - 1)
        def _():
            hop(batch).wait_send()

        return carry

    lax.fori_loop(0, batches, finish, 0)

    def drain(other, carry):
        owner = 2 * other + core
        for slot in range(kept):
            block = held(0, slot, owner, side)

            @pl.when(jnp.logical_and(other <= chip, chip < chips - 1))
            def _():
                along(slot, block, owner, 1, up_send).wait_send()

            @pl.when(jnp.logical_and(other >= chip, chip > 0))
            def _():
                along(slot, block, owner, -1, down_send).wait_send()

            @pl.when(other != chip)
            def _():
                direct(slot, half_shard(1, slot), me, owner).wait_send()
                to_mate(slot, owner).wait_send()
                for which in range(2):
                    to_pair(slot, owner, which).wait_send()

            @pl.when(other == chip)
            def _():
                shard_to_pair(slot, whole_shard(slot), owner).wait_send()

        return carry

    lax.fori_loop(0, chips, drain, 0)


def staged(features, weights, history, own_adj, side_adj, hist_adj, send_ids, hist_ids):
    segments = lax.axis_size("segment")
    places = lax.axis_size("graph")
    layer_total, shard, width = weights.shape
    kept = layer_total // segments
    batches, rows = own_adj.shape[0], own_adj.shape[2]
    edges = side_adj.shape[1] * side_adj.shape[2]
    chips = places // 2
    dma = pltpu.SemaphoreType.DMA

    def kernel(*refs):
        stage_kernel(segments, places, layer_total, *refs)

    anywhere = pl.BlockSpec(memory_space=pl.ANY)
    half = jnp.bfloat16
    return pl.pallas_call(
        kernel,
        out_shape=jax.ShapeDtypeStruct((kept, batches * rows, width), half),
        in_specs=[anywhere] * 8,
        out_specs=pl.BlockSpec(memory_space=pltpu.VMEM),
        scratch_shapes=[
            pltpu.VMEM(features.shape, half),
            pltpu.VMEM((kept,) + history.shape[1:], half),
            pltpu.VMEM(own_adj.shape, half),
            pltpu.VMEM((batches, edges, rows), half),
            pltpu.VMEM(hist_adj.shape, half),
            pltpu.VMEM(send_ids.shape, send_ids.dtype),
            pltpu.VMEM(hist_ids.shape, hist_ids.dtype),
            pltpu.VMEM((2, kept, places * shard, width), half),
            pltpu.VMEM((kept, batches, rows, width), jnp.float32),
            pltpu.VMEM((batches, edges, rows), half),
            pltpu.VMEM((batches, rows, width), half),
            pltpu.VMEM((kept, batches, edges, width), half),
            pltpu.VMEM((kept, batches, edges, width), half),
            dma((7,)),
            dma((kept,)),
            dma((2, kept, chips)),
            dma((kept, chips)),
            dma((kept, 2, chips)),
            dma((kept,)),
            dma((kept, chips)),
            dma((kept, chips)),
            dma((kept, chips)),
            dma((kept, chips)),
            dma((kept, 2, chips)),
            dma((kept,)),
            dma((kept, batches, len(OFFSETS))),
            dma((kept, batches, len(OFFSETS))),
            dma((batches,)),
            dma((batches,)),
        ],
        compiler_params=pltpu.CompilerParams(
            collective_id=0, has_side_effects=True, vmem_limit_bytes=60 * 1024 * 1024
        ),
    )(
        features,
        weights,
        history,
        own_adj,
        side_adj.reshape(batches, edges, rows),
        hist_adj,
        send_ids,
        hist_ids,
    )


def device_part(features, weights, *rest):
    places, segments = lax.axis_size("graph"), lax.axis_size("segment")
    whole_tiles = weights.shape[1] % (2 * TILE_ROWS) == 0 and rest[2].shape[2] % TILE_ROWS == 0
    even = places % 2 == 0 and segments % 2 == 0 and weights.shape[0] % segments == 0
    if whole_tiles and even:
        return staged(features, weights, *rest)
    return shards(features, weights, *rest)


def solution(mesh):
    in_specs = (
        P("graph", None),
        P(None, "graph", None),
        P(None, "graph", None),
        P(None, "graph", None),
        P(None, None, "graph", None),
        P(None, "graph", None),
        P(None, None, "graph"),
        P(None, "graph"),
    )
    out_specs = P("segment", "graph", None)
    return jax.shard_map(device_part, mesh=mesh, in_specs=in_specs, out_specs=out_specs, check_vma=False)
```

```python
import math

import jax
import jax.numpy as jnp
from jax import lax
from jax.experimental import pallas as pl
from jax.experimental.pallas import tpu as pltpu
from jax.sharding import PartitionSpec as P

ALPHA = 0.1
LAMBDA = 1.5
OFFSETS = (1, -1, 2, -2)


def shifted(value, axis, steps):
    count = lax.axis_size(axis)
    initial, last = (max(0, -steps), min(count, count - steps))
    return lax.ppermute(value, axis, [(source, source + steps) for source in range(initial, last)])


def propagate(
    current, initial, layer_number, weight, tables, own_tile, side_tile, send_rows, past_rows
):
    edge_count = send_rows.shape[1]
    picked = jnp.take(current, send_rows.reshape(-1), axis=0)
    arrived = []
    for direction in range(len(OFFSETS)):
        outgoing = picked[direction * edge_count : (direction + 1) * edge_count]
        arrived.append(shifted(outgoing, "graph", OFFSETS[direction]))
    layer_table = lax.dynamic_index_in_dim(tables, layer_number, 0, keepdims=False)
    arrived.append(jnp.take(layer_table, past_rows, axis=0))
    gathered_rows = jnp.concatenate(arrived, axis=0)
    aggregate = jnp.dot(own_tile, current, preferred_element_type=jnp.float32)
    aggregate = aggregate + lax.dot_general(
        side_tile, gathered_rows, (((0,), (0,)), ((), ())), preferred_element_type=jnp.float32
    )
    support = (1.0 - ALPHA) * aggregate + ALPHA * initial.astype(jnp.float32)
    mixing = jnp.dot(support.astype(jnp.bfloat16), weight, preferred_element_type=jnp.float32)
    strength = jnp.log(LAMBDA / (layer_number.astype(jnp.float32) + 1.0) + 1.0)
    return jax.nn.relu((1.0 - strength) * support + strength * mixing).astype(jnp.bfloat16)


def batch_tiles(own_adj, side_adj, hist_adj, send_ids, hist_ids, batch_safe):
    batch_rows = own_adj.shape[2]
    side_edges = side_adj.shape[1] * side_adj.shape[2]
    own_tile = lax.dynamic_index_in_dim(own_adj, batch_safe, 0, keepdims=False)
    edge_tile = lax.dynamic_index_in_dim(side_adj, batch_safe, 0, keepdims=False).reshape(
        side_edges, batch_rows
    )
    past_tile = lax.dynamic_index_in_dim(hist_adj, batch_safe, 0, keepdims=False)
    side_tile = jnp.concatenate([edge_tile, past_tile], axis=0)
    send_rows = lax.dynamic_index_in_dim(send_ids, batch_safe, 0, keepdims=False)
    past_rows = lax.dynamic_index_in_dim(hist_ids, batch_safe, 0, keepdims=False)
    return (own_tile, side_tile, send_rows, past_rows)


def shards(features, weights, history, own_adj, side_adj, hist_adj, send_ids, hist_ids):
    segment_pos = lax.axis_index("segment")
    segment_count = lax.axis_size("segment")
    batch_count = own_adj.shape[0]
    batch_rows = own_adj.shape[2]
    layer_total = weights.shape[0]
    kept_slots = layer_total // segment_count
    initial = lax.dynamic_slice_in_dim(features, segment_pos * batch_rows, batch_rows, 0)
    own_tile, side_tile, send_rows, past_rows = batch_tiles(
        own_adj, side_adj, hist_adj, send_ids, hist_ids, segment_pos
    )
    current = initial
    produced = []
    for number in range(layer_total):
        weight = lax.all_gather(weights[number], "graph", axis=0, tiled=True)
        current = propagate(
            current,
            initial,
            jnp.int32(number),
            weight,
            history,
            own_tile,
            side_tile,
            send_rows,
            past_rows,
        )
        produced.append(current)
    arranged = jnp.stack(
        [
            jnp.stack([produced[kept_slots * target + slot] for target in range(segment_count)])
            for slot in range(kept_slots)
        ]
    )
    received = lax.all_to_all(arranged, "segment", split_axis=1, concat_axis=1, tiled=True)
    return received.reshape(kept_slots, batch_count * batch_rows, features.shape[1])


TILE_ROWS = 16
MESH = pl.DeviceIdType.MESH


def column_of(row):
    count = row.shape[1]
    down = lax.broadcasted_iota(jnp.int32, (count, count), 0)
    across = lax.broadcasted_iota(jnp.int32, (count, count), 1)
    spread = jnp.broadcast_to(row.astype(jnp.float32), (count, count))
    return jnp.sum(jnp.where(down == across, spread, 0.0), axis=1, keepdims=True)


def selector(row, width):
    across = lax.broadcasted_iota(jnp.int32, (row.shape[1], width), 1).astype(jnp.float32)
    return jnp.where(across == column_of(row), 1.0, 0.0).astype(jnp.bfloat16)


def transposed_dot(left, right):
    return lax.dot_general(
        left, right, (((0,), (0,)), ((), ())), preferred_element_type=jnp.float32
    )


def stage_kernel(
    segments, places, layer_total,
    features_in, weights, history_in, own_in, side_in, hist_in, send_in, ids_in,
    out,
    features, history, own_adj, side_adj, hist_adj, send_ids, hist_ids,
    full, base, select, entering, leaving, arrived,
    load_sem, own_sem, line_recv, mate_recv, pair_recv, shard_recv,
    up_send, down_send, up_whole, down_whole, mate_send, pair_send, shard_send,
    edge_send, edge_recv, hop_send, hop_recv,
):
    seg = lax.axis_index("segment")
    me = lax.axis_index("graph")
    kept = layer_total // segments
    batches, rows = own_adj.shape[0], own_adj.shape[2]
    shard = weights.shape[1]
    piece = shard // 2
    edge = send_ids.shape[2]
    chips = places // 2
    chip = me // 2
    core = me % 2
    pair = me + 1 - 2 * core
    half = segments // 2
    side = seg // half
    mate = seg + half - 2 * half * side
    first_layer = seg * kept

    loads = [
        pltpu.make_async_copy(source, target, load_sem.at[number])
        for number, (source, target) in enumerate(
            [
                (features_in, features),
                (history_in.at[pl.ds(first_layer, kept)], history),
                (own_in, own_adj),
                (side_in, side_adj),
                (hist_in, hist_adj),
                (send_in, send_ids),
                (ids_in, hist_ids),
            ]
        )
    ]
    for load in loads:
        load.start()

    barrier = pltpu.get_barrier_semaphore()
    expected = jnp.int32(1)
    pl.semaphore_signal(barrier, inc=1, device_id={"segment": mate}, device_id_type=MESH)
    for offset in OFFSETS:
        there = me + offset
        inside = jnp.logical_and(there >= 0, there < places)

        @pl.when(inside)
        def _():
            pl.semaphore_signal(barrier, inc=1, device_id={"graph": there}, device_id_type=MESH)

        expected = expected + inside.astype(jnp.int32)
    for step in (1, -1):
        beside = seg + step
        inside = jnp.logical_and(beside >= 0, beside < segments)

        @pl.when(inside)
        def _():
            pl.semaphore_signal(
                barrier, inc=1, device_id={"segment": beside}, device_id_type=MESH
            )

        expected = expected + inside.astype(jnp.int32)
    pl.semaphore_wait(barrier, expected)


    def shard_rows(owner):
        return pl.ds(pl.multiple_of(owner * shard, shard), shard)

    def piece_rows(owner, which):
        return pl.ds(pl.multiple_of(owner * shard + which * piece, piece), piece)

    def whole_shard(slot):
        return weights.at[first_layer + slot]

    def own_copy(slot):
        return pltpu.make_async_copy(
            whole_shard(slot), full.at[side, slot, shard_rows(me)], own_sem.at[slot]
        )

    def push(turn, slot, source, owner, which, target, send_sem, recv_sem):
        return pltpu.make_async_remote_copy(
            src_ref=source,
            dst_ref=full.at[turn, slot, piece_rows(owner, which)],
            send_sem=send_sem,
            recv_sem=recv_sem,
            device_id=target,
            device_id_type=MESH,
        )

    def held(turn, slot, owner, which):
        return full.at[turn, slot, piece_rows(owner, which)]

    def along(slot, source, owner, step, send_sem):
        return push(
            0, slot, source, owner, side, {"graph": me + 2 * step},
            send_sem.at[slot, owner // 2], line_recv.at[0, slot, owner // 2],
        )

    def along_whole(slot, source, owner, step, send_sem):
        return pltpu.make_async_remote_copy(
            src_ref=source,
            dst_ref=full.at[1, slot, shard_rows(owner)],
            send_sem=send_sem.at[slot, owner // 2],
            recv_sem=line_recv.at[1, slot, owner // 2],
            device_id={"graph": me + 2 * step},
            device_id_type=MESH,
        )

    def whole_to_pair(slot, owner):
        block = full.at[1, slot, shard_rows(owner)]
        return pltpu.make_async_remote_copy(
            src_ref=block,
            dst_ref=block,
            send_sem=pair_send.at[slot, 0, owner // 2],
            recv_sem=pair_recv.at[slot, 0, owner // 2],
            device_id={"graph": pair},
            device_id_type=MESH,
        )

    def to_pair(slot, owner, which):
        return push(
            side, slot, held(side, slot, owner, which), owner, which, {"graph": pair},
            pair_send.at[slot, which, owner // 2], pair_recv.at[slot, which, owner // 2],
        )

    def to_mate(slot, owner):
        turn = 1 - side
        return push(
            turn, slot, held(turn, slot, owner, side), owner, side, {"segment": mate},
            mate_send.at[slot, owner // 2], mate_recv.at[slot, owner // 2],
        )

    def from_mate(slot, owner):
        which = 1 - side
        return push(
            side, slot, held(side, slot, owner, which), owner, which, {"segment": mate},
            mate_send.at[slot, owner // 2], mate_recv.at[slot, owner // 2],
        )

    def shard_to_pair(slot, source, owner):
        return pltpu.make_async_remote_copy(
            src_ref=source,
            dst_ref=full.at[side, slot, shard_rows(owner)],
            send_sem=shard_send.at[slot],
            recv_sem=shard_recv.at[slot],
            device_id={"graph": pair},
            device_id_type=MESH,
        )

    def half_shard(turn, slot):
        number = (seg + (turn - side) * half) * kept + slot
        return weights.at[number, pl.ds(pl.multiple_of(side * piece, piece), piece)]

    def place_own(turn, slot):
        @pl.when(side == turn)
        def _():
            shard_to_pair(slot, whole_shard(slot), me).start()
            own_copy(slot).start()

    def open_slot(slot):
        source = half_shard(0, slot)

        @pl.when(chip < chips - 1)
        def _():
            along(slot, source, me, 1, up_send).start()

        @pl.when(chip > 0)
        def _():
            along(slot, source, me, -1, down_send).start()

        place_own(0, slot)

    def open_whole(slot):
        source = whole_shard(slot)

        @pl.when(chip < chips - 1)
        def _():
            along_whole(slot, source, me, 1, up_whole).start()

        @pl.when(chip > 0)
        def _():
            along_whole(slot, source, me, -1, down_whole).start()

        place_own(1, slot)

    def relay_whole(slot, distance):
        below = me - 2 * distance

        @pl.when(below >= 0)
        def _():
            block = full.at[1, slot, shard_rows(below)]
            along_whole(slot, block, below, 1, up_whole).wait_recv()

            @pl.when(chip < chips - 1)
            def _():
                along_whole(slot, block, below, 1, up_whole).start()

            whole_to_pair(slot, below).start()

        above = me + 2 * distance

        @pl.when(above < places)
        def _():
            block = full.at[1, slot, shard_rows(above)]
            along_whole(slot, block, above, -1, down_whole).wait_recv()

            @pl.when(chip > 0)
            def _():
                along_whole(slot, block, above, -1, down_whole).start()

            whole_to_pair(slot, above).start()

    def hand_on(turn, slot, owner):
        @pl.when(side == turn)
        def _():
            to_pair(slot, owner, side).start()

        @pl.when(side != turn)
        def _():
            to_mate(slot, owner).start()

    def relay(slot, distance):
        below = me - 2 * distance

        @pl.when(below >= 0)
        def _():
            block = held(0, slot, below, side)
            along(slot, block, below, 1, up_send).wait_recv()

            @pl.when(chip < chips - 1)
            def _():
                along(slot, block, below, 1, up_send).start()

            hand_on(0, slot, below)

        above = me + 2 * distance

        @pl.when(above < places)
        def _():
            block = held(0, slot, above, side)
            along(slot, block, above, -1, down_send).wait_recv()

            @pl.when(chip > 0)
            def _():
                along(slot, block, above, -1, down_send).start()

            hand_on(0, slot, above)

    def bridge(slot, distance):
        for owner in (me - 2 * distance, me + 2 * distance):

            @pl.when(jnp.logical_and(owner >= 0, owner < places))
            def _():
                from_mate(slot, owner).wait_recv()
                to_pair(slot, owner, 1 - side).start()

    def close_slot(slot):
        own_copy(slot).wait()
        shard_to_pair(slot, full.at[side, slot, shard_rows(pair)], pair).wait_recv()

        def from_pair(other, carry):
            @pl.when(other != chip)
            def _():
                owner = 2 * other + 1 - core

                @pl.when(side == 0)
                def _():
                    for which in range(2):
                        to_pair(slot, owner, which).wait_recv()

                @pl.when(side == 1)
                def _():
                    whole_to_pair(slot, owner).wait_recv()

            return carry

        lax.fori_loop(0, chips, from_pair, 0)

    def edge_copy(slot, batch, direction):
        part = pl.ds(direction * edge, edge)
        return pltpu.make_async_remote_copy(
            src_ref=leaving.at[slot, batch, part],
            dst_ref=arrived.at[slot, batch, part],
            send_sem=edge_send.at[slot, batch, direction],
            recv_sem=edge_recv.at[slot, batch, direction],
            device_id={"graph": me + OFFSETS[direction]},
            device_id_type=MESH,
        )

    def sends(direction):
        there = me + OFFSETS[direction]
        return jnp.logical_and(there >= 0, there < places)

    def receives(direction):
        there = me - OFFSETS[direction]
        return jnp.logical_and(there >= 0, there < places)

    def send_edges(slot, batch, current):
        leaving[slot, batch] = jnp.dot(
            select[batch], current, preferred_element_type=jnp.float32
        ).astype(jnp.bfloat16)
        for direction in range(len(OFFSETS)):

            @pl.when(sends(direction))
            def _():
                edge_copy(slot, batch, direction).start()

    def batch_range(batch):
        return pl.ds(pl.multiple_of(batch * rows, rows), rows)

    def hop(batch):
        return pltpu.make_async_remote_copy(
            src_ref=out.at[kept - 1, batch_range(batch)],
            dst_ref=entering.at[batch],
            send_sem=hop_send.at[batch],
            recv_sem=hop_recv.at[batch],
            device_id={"segment": seg + 1},
            device_id_type=MESH,
        )

    def prepare(batch, carry):
        for direction in range(len(OFFSETS)):
            part = pl.ds(direction * edge, edge)
            select[batch, part] = selector(
                send_ids[batch, pl.ds(direction, 1), :], rows
            )
            for slot in range(kept):

                @pl.when(jnp.logical_not(receives(direction)))
                def _():
                    arrived[slot, batch, part] = jnp.zeros(
                        (edge, arrived.shape[3]), jnp.bfloat16
                    )

        initial = features[batch_range(batch), :]

        @pl.when(seg == 0)
        def _():
            entering[batch] = initial

        lookup = selector(hist_ids[pl.ds(batch, 1), :], history.shape[1])
        for slot in range(kept):
            looked = jnp.dot(
                lookup, history[slot], preferred_element_type=jnp.float32
            ).astype(jnp.bfloat16)
            past = transposed_dot(hist_adj[batch], looked)
            base[slot, batch] = (1.0 - ALPHA) * past + ALPHA * initial.astype(jnp.float32)
        return carry

    def layer(slot, batch):
        strength = jnp.float32(0.0)
        for number in range(layer_total):
            value = math.log(LAMBDA / (number + 1.0) + 1.0)
            strength = jnp.where(first_layer + slot == number, jnp.float32(value), strength)
        if slot == 0:
            current = entering[batch]
        else:
            current = out[slot - 1, batch_range(batch), :]
        aggregate = jnp.dot(own_adj[batch], current, preferred_element_type=jnp.float32)
        for direction in range(len(OFFSETS)):

            @pl.when(receives(direction))
            def _():
                edge_copy(slot, batch, direction).wait_recv()

        aggregate = aggregate + transposed_dot(side_adj[batch], arrived[slot, batch])
        support = (1.0 - ALPHA) * aggregate + base[slot, batch]
        mixing = jnp.dot(
            support.astype(jnp.bfloat16), full[side, slot], preferred_element_type=jnp.float32
        )
        result = jnp.maximum((1.0 - strength) * support + strength * mixing, 0.0)
        result = result.astype(jnp.bfloat16)
        out[slot, batch_range(batch), :] = result
        if slot < kept - 1:
            send_edges(slot + 1, batch, result)
        else:

            @pl.when(seg < segments - 1)
            def _():
                hop(batch).start()

    far = chips - 1

    def line_steps(slot):
        steps = []
        for distance in range(1, chips):
            work = [(relay, (slot, distance))]
            if distance == max(1, far - 1) and slot < kept - 1:
                work.append((open_slot, (slot + 1,)))
            if distance > 1:
                work.append((bridge, (slot, distance - 1)))
            steps.append(work)
        steps.append([(bridge, (slot, far))])
        return steps

    def run(work):
        for action, arguments in work:
            if action is bridge:

                @pl.when(side == 0)
                def _():
                    action(*arguments)

            else:
                action(*arguments)

    open_slot(0)
    for load in loads:
        load.wait()
    middle = batches // 2
    lax.fori_loop(0, middle, prepare, 0)
    for number, work in enumerate(line_steps(0)):
        if number == far and kept > 1:
            relay(1, 1)
        run(work)
        if number == 0:
            lax.fori_loop(middle, batches, prepare, 0)

            @pl.when(seg == 0)
            def _():
                def early(batch, carry):
                    send_edges(0, batch, entering[batch])
                    return carry

                lax.fori_loop(0, batches, early, 0)

    first_tasks = [[] for _ in range(batches * kept)]
    others = []
    for slot in range(1, kept):
        steps = line_steps(slot)
        if slot == 1:
            steps[0] = steps[0][1:]
            steps = [steps[0] + steps[1]] + steps[2:] if far > 1 else steps
        others += steps
        for number, work in enumerate(steps):
            first_tasks[min((slot - 1) * batches + number, slot * batches - 1)] += work

    @pl.when(seg > 0)
    def _():
        for number, work in enumerate(others):
            run(work)
            if number == 0:

                @pl.when(side == 1)
                def _():
                    open_whole(0)

    @pl.when(side == 1)
    def _():
        if not others:
            open_whole(0)
        for slot in range(kept):
            for distance in range(1, chips):
                relay_whole(slot, distance)
                if slot < kept - 1 and distance == max(1, far - 1):
                    open_whole(slot + 1)

    lag = jnp.where(seg == 0, batches, 1)
    ticks = batches + lag * (kept - 1)

    def tick(time, carry):
        @pl.when(jnp.logical_and(seg > 0, time < batches))
        def _():
            hop(time).wait_recv()
            send_edges(0, time, entering[time])

        for number, work in enumerate(first_tasks):
            if work:

                @pl.when(jnp.logical_and(seg == 0, time == number))
                def _():
                    run(work)

        for slot in range(kept - 1, -1, -1):

            @pl.when(time == lag * slot)
            def _():
                close_slot(slot)

            batch = time - lag * slot

            @pl.when(jnp.logical_and(batch >= 0, batch < batches))
            def _():
                layer(slot, batch)

        return carry

    lax.fori_loop(0, ticks, tick, 0)

    def finish(batch, carry):
        for slot in range(kept):
            for direction in range(len(OFFSETS)):

                @pl.when(sends(direction))
                def _():
                    edge_copy(slot, batch, direction).wait_send()

        @pl.when(seg < segments - 1)
        def _():
            hop(batch).wait_send()

        return carry

    lax.fori_loop(0, batches, finish, 0)

    def drain(other, carry):
        owner = 2 * other + core
        for slot in range(kept):
            block = held(0, slot, owner, side)

            @pl.when(jnp.logical_and(other <= chip, chip < chips - 1))
            def _():
                along(slot, block, owner, 1, up_send).wait_send()

                @pl.when(side == 1)
                def _():
                    along_whole(slot, whole_shard(slot), owner, 1, up_whole).wait_send()

            @pl.when(jnp.logical_and(other >= chip, chip > 0))
            def _():
                along(slot, block, owner, -1, down_send).wait_send()

                @pl.when(side == 1)
                def _():
                    along_whole(slot, whole_shard(slot), owner, -1, down_whole).wait_send()

            @pl.when(other != chip)
            def _():
                @pl.when(side == 0)
                def _():
                    for which in range(2):
                        to_pair(slot, owner, which).wait_send()

                @pl.when(side == 1)
                def _():
                    to_mate(slot, owner).wait_send()
                    whole_to_pair(slot, owner).wait_send()

            @pl.when(other == chip)
            def _():
                shard_to_pair(slot, whole_shard(slot), owner).wait_send()

        return carry

    lax.fori_loop(0, chips, drain, 0)


def staged(features, weights, history, own_adj, side_adj, hist_adj, send_ids, hist_ids):
    segments = lax.axis_size("segment")
    places = lax.axis_size("graph")
    layer_total, shard, width = weights.shape
    kept = layer_total // segments
    batches, rows = own_adj.shape[0], own_adj.shape[2]
    edges = side_adj.shape[1] * side_adj.shape[2]
    chips = places // 2
    dma = pltpu.SemaphoreType.DMA

    def kernel(*refs):
        stage_kernel(segments, places, layer_total, *refs)

    anywhere = pl.BlockSpec(memory_space=pl.ANY)
    half = jnp.bfloat16
    return pl.pallas_call(
        kernel,
        out_shape=jax.ShapeDtypeStruct((kept, batches * rows, width), half),
        in_specs=[anywhere] * 8,
        out_specs=pl.BlockSpec(memory_space=pltpu.VMEM),
        scratch_shapes=[
            pltpu.VMEM(features.shape, half),
            pltpu.VMEM((kept,) + history.shape[1:], half),
            pltpu.VMEM(own_adj.shape, half),
            pltpu.VMEM((batches, edges, rows), half),
            pltpu.VMEM(hist_adj.shape, half),
            pltpu.VMEM(send_ids.shape, send_ids.dtype),
            pltpu.VMEM(hist_ids.shape, hist_ids.dtype),
            pltpu.VMEM((2, kept, places * shard, width), half),
            pltpu.VMEM((kept, batches, rows, width), jnp.float32),
            pltpu.VMEM((batches, edges, rows), half),
            pltpu.VMEM((batches, rows, width), half),
            pltpu.VMEM((kept, batches, edges, width), half),
            pltpu.VMEM((kept, batches, edges, width), half),
            dma((7,)),
            dma((kept,)),
            dma((2, kept, chips)),
            dma((kept, chips)),
            dma((kept, 2, chips)),
            dma((kept,)),
            dma((kept, chips)),
            dma((kept, chips)),
            dma((kept, chips)),
            dma((kept, chips)),
            dma((kept, chips)),
            dma((kept, 2, chips)),
            dma((kept,)),
            dma((kept, batches, len(OFFSETS))),
            dma((kept, batches, len(OFFSETS))),
            dma((batches,)),
            dma((batches,)),
        ],
        compiler_params=pltpu.CompilerParams(
            collective_id=0, has_side_effects=True, vmem_limit_bytes=60 * 1024 * 1024
        ),
    )(
        features,
        weights,
        history,
        own_adj,
        side_adj.reshape(batches, edges, rows),
        hist_adj,
        send_ids,
        hist_ids,
    )


def device_part(features, weights, *rest):
    places, segments = lax.axis_size("graph"), lax.axis_size("segment")
    whole_tiles = weights.shape[1] % (2 * TILE_ROWS) == 0 and rest[2].shape[2] % TILE_ROWS == 0
    even = places % 2 == 0 and segments % 2 == 0 and weights.shape[0] % segments == 0
    if whole_tiles and even:
        return staged(features, weights, *rest)
    return shards(features, weights, *rest)


def solution(mesh):
    in_specs = (
        P("graph", None),
        P(None, "graph", None),
        P(None, "graph", None),
        P(None, "graph", None),
        P(None, None, "graph", None),
        P(None, "graph", None),
        P(None, None, "graph"),
        P(None, "graph"),
    )
    out_specs = P("segment", "graph", None)
    return jax.shard_map(device_part, mesh=mesh, in_specs=in_specs, out_specs=out_specs, check_vma=False)
```

```python
import math

import jax
import jax.numpy as jnp
from jax import lax
from jax.experimental import pallas as pl
from jax.experimental.pallas import tpu as pltpu
from jax.sharding import PartitionSpec as P

ALPHA = 0.1
LAMBDA = 1.5
OFFSETS = (1, -1, 2, -2)


def shifted(value, axis, steps):
    count = lax.axis_size(axis)
    initial, last = (max(0, -steps), min(count, count - steps))
    return lax.ppermute(value, axis, [(source, source + steps) for source in range(initial, last)])


def propagate(
    current, initial, layer_number, weight, tables, own_tile, side_tile, send_rows, past_rows
):
    edge_count = send_rows.shape[1]
    picked = jnp.take(current, send_rows.reshape(-1), axis=0)
    arrived = []
    for direction in range(len(OFFSETS)):
        outgoing = picked[direction * edge_count : (direction + 1) * edge_count]
        arrived.append(shifted(outgoing, "graph", OFFSETS[direction]))
    layer_table = lax.dynamic_index_in_dim(tables, layer_number, 0, keepdims=False)
    arrived.append(jnp.take(layer_table, past_rows, axis=0))
    gathered_rows = jnp.concatenate(arrived, axis=0)
    aggregate = jnp.dot(own_tile, current, preferred_element_type=jnp.float32)
    aggregate = aggregate + lax.dot_general(
        side_tile, gathered_rows, (((0,), (0,)), ((), ())), preferred_element_type=jnp.float32
    )
    support = (1.0 - ALPHA) * aggregate + ALPHA * initial.astype(jnp.float32)
    mixing = jnp.dot(support.astype(jnp.bfloat16), weight, preferred_element_type=jnp.float32)
    strength = jnp.log(LAMBDA / (layer_number.astype(jnp.float32) + 1.0) + 1.0)
    return jax.nn.relu((1.0 - strength) * support + strength * mixing).astype(jnp.bfloat16)


def batch_tiles(own_adj, side_adj, hist_adj, send_ids, hist_ids, batch_safe):
    batch_rows = own_adj.shape[2]
    side_edges = side_adj.shape[1] * side_adj.shape[2]
    own_tile = lax.dynamic_index_in_dim(own_adj, batch_safe, 0, keepdims=False)
    edge_tile = lax.dynamic_index_in_dim(side_adj, batch_safe, 0, keepdims=False).reshape(
        side_edges, batch_rows
    )
    past_tile = lax.dynamic_index_in_dim(hist_adj, batch_safe, 0, keepdims=False)
    side_tile = jnp.concatenate([edge_tile, past_tile], axis=0)
    send_rows = lax.dynamic_index_in_dim(send_ids, batch_safe, 0, keepdims=False)
    past_rows = lax.dynamic_index_in_dim(hist_ids, batch_safe, 0, keepdims=False)
    return (own_tile, side_tile, send_rows, past_rows)


def shards(features, weights, history, own_adj, side_adj, hist_adj, send_ids, hist_ids):
    segment_pos = lax.axis_index("segment")
    segment_count = lax.axis_size("segment")
    batch_count = own_adj.shape[0]
    batch_rows = own_adj.shape[2]
    layer_total = weights.shape[0]
    kept_slots = layer_total // segment_count
    initial = lax.dynamic_slice_in_dim(features, segment_pos * batch_rows, batch_rows, 0)
    own_tile, side_tile, send_rows, past_rows = batch_tiles(
        own_adj, side_adj, hist_adj, send_ids, hist_ids, segment_pos
    )
    current = initial
    produced = []
    for number in range(layer_total):
        weight = lax.all_gather(weights[number], "graph", axis=0, tiled=True)
        current = propagate(
            current,
            initial,
            jnp.int32(number),
            weight,
            history,
            own_tile,
            side_tile,
            send_rows,
            past_rows,
        )
        produced.append(current)
    arranged = jnp.stack(
        [
            jnp.stack([produced[kept_slots * target + slot] for target in range(segment_count)])
            for slot in range(kept_slots)
        ]
    )
    received = lax.all_to_all(arranged, "segment", split_axis=1, concat_axis=1, tiled=True)
    return received.reshape(kept_slots, batch_count * batch_rows, features.shape[1])


TILE_ROWS = 16
TILE_COLUMNS = 128
HALVES = 2
MESH = pl.DeviceIdType.MESH


def column_of(row):
    count = row.shape[1]
    down = lax.broadcasted_iota(jnp.int32, (count, count), 0)
    across = lax.broadcasted_iota(jnp.int32, (count, count), 1)
    spread = jnp.broadcast_to(row.astype(jnp.float32), (count, count))
    return jnp.sum(jnp.where(down == across, spread, 0.0), axis=1, keepdims=True)


def selector(row, width):
    across = lax.broadcasted_iota(jnp.int32, (row.shape[1], width), 1).astype(jnp.float32)
    return jnp.where(across == column_of(row), 1.0, 0.0).astype(jnp.bfloat16)


def transposed_dot(left, right):
    return lax.dot_general(
        left, right, (((0,), (0,)), ((), ())), preferred_element_type=jnp.float32
    )


def stage_kernel(
    segments, places, layer_total,
    features_in, weights, history_in, own_in, side_in, hist_in, send_in, ids_in,
    out,
    features, history, own_adj, side_adj, hist_adj, send_ids, hist_ids,
    full, base, select, entering, leaving, arrived,
    load_sem, own_sem, line_recv, mate_recv, pair_recv, shard_recv,
    up_send, down_send, up_whole, down_whole, mate_send, pair_send, shard_send,
    edge_send, edge_recv, hop_send, hop_recv,
):
    seg = lax.axis_index("segment")
    me = lax.axis_index("graph")
    kept = layer_total // segments
    batches, rows = own_adj.shape[0], own_adj.shape[2]
    shard = weights.shape[1]
    piece = shard // 2
    edge = send_ids.shape[2]
    chips = places // 2
    chip = me // 2
    core = me % 2
    pair = me + 1 - 2 * core
    half = segments // 2
    side = seg // half
    mate = seg + half - 2 * half * side
    first_layer = seg * kept

    loads = [
        pltpu.make_async_copy(source, target, load_sem.at[number])
        for number, (source, target) in enumerate(
            [
                (features_in, features),
                (history_in.at[pl.ds(first_layer, kept)], history),
                (own_in, own_adj),
                (side_in, side_adj),
                (hist_in, hist_adj),
                (send_in, send_ids),
                (ids_in, hist_ids),
            ]
        )
    ]
    for load in loads:
        load.start()

    barrier = pltpu.get_barrier_semaphore()
    expected = jnp.int32(1)
    pl.semaphore_signal(barrier, inc=1, device_id={"segment": mate}, device_id_type=MESH)
    for offset in OFFSETS:
        there = me + offset
        inside = jnp.logical_and(there >= 0, there < places)

        @pl.when(inside)
        def _():
            pl.semaphore_signal(barrier, inc=1, device_id={"graph": there}, device_id_type=MESH)

        expected = expected + inside.astype(jnp.int32)
    for step in (1, -1):
        beside = seg + step
        inside = jnp.logical_and(beside >= 0, beside < segments)

        @pl.when(inside)
        def _():
            pl.semaphore_signal(
                barrier, inc=1, device_id={"segment": beside}, device_id_type=MESH
            )

        expected = expected + inside.astype(jnp.int32)
    pl.semaphore_wait(barrier, expected)


    def shard_rows(owner):
        return pl.ds(pl.multiple_of(owner * shard, shard), shard)

    def piece_rows(owner, which):
        return pl.ds(pl.multiple_of(owner * shard + which * piece, piece), piece)

    def whole_shard(slot):
        return weights.at[first_layer + slot]

    def own_copy(slot):
        return pltpu.make_async_copy(
            whole_shard(slot), full.at[side, slot, shard_rows(me)], own_sem.at[slot]
        )

    def push(turn, slot, source, owner, which, target, send_sem, recv_sem):
        return pltpu.make_async_remote_copy(
            src_ref=source,
            dst_ref=full.at[turn, slot, piece_rows(owner, which)],
            send_sem=send_sem,
            recv_sem=recv_sem,
            device_id=target,
            device_id_type=MESH,
        )

    def held(turn, slot, owner, which):
        return full.at[turn, slot, piece_rows(owner, which)]

    def along(slot, source, owner, step, send_sem):
        return push(
            0, slot, source, owner, side, {"graph": me + 2 * step},
            send_sem.at[slot, owner // 2], line_recv.at[0, slot, owner // 2],
        )

    def along_whole(slot, source, owner, step, send_sem):
        return pltpu.make_async_remote_copy(
            src_ref=source,
            dst_ref=full.at[1, slot, shard_rows(owner)],
            send_sem=send_sem.at[slot, owner // 2],
            recv_sem=line_recv.at[1, slot, owner // 2],
            device_id={"graph": me + 2 * step},
            device_id_type=MESH,
        )

    def whole_to_pair(slot, owner):
        block = full.at[1, slot, shard_rows(owner)]
        return pltpu.make_async_remote_copy(
            src_ref=block,
            dst_ref=block,
            send_sem=pair_send.at[slot, 0, owner // 2],
            recv_sem=pair_recv.at[slot, 0, owner // 2],
            device_id={"graph": pair},
            device_id_type=MESH,
        )

    def to_pair(slot, owner, which):
        return push(
            side, slot, held(side, slot, owner, which), owner, which, {"graph": pair},
            pair_send.at[slot, which, owner // 2], pair_recv.at[slot, which, owner // 2],
        )

    def to_mate(slot, owner):
        turn = 1 - side
        return push(
            turn, slot, held(turn, slot, owner, side), owner, side, {"segment": mate},
            mate_send.at[slot, owner // 2], mate_recv.at[slot, owner // 2],
        )

    def from_mate(slot, owner):
        which = 1 - side
        return push(
            side, slot, held(side, slot, owner, which), owner, which, {"segment": mate},
            mate_send.at[slot, owner // 2], mate_recv.at[slot, owner // 2],
        )

    def shard_to_pair(slot, source, owner):
        return pltpu.make_async_remote_copy(
            src_ref=source,
            dst_ref=full.at[side, slot, shard_rows(owner)],
            send_sem=shard_send.at[slot],
            recv_sem=shard_recv.at[slot],
            device_id={"graph": pair},
            device_id_type=MESH,
        )

    def half_shard(turn, slot):
        number = (seg + (turn - side) * half) * kept + slot
        return weights.at[number, pl.ds(pl.multiple_of(side * piece, piece), piece)]

    def place_own(turn, slot):
        @pl.when(side == turn)
        def _():
            shard_to_pair(slot, whole_shard(slot), me).start()
            own_copy(slot).start()

    def open_slot(slot):
        source = half_shard(0, slot)

        @pl.when(chip < chips - 1)
        def _():
            along(slot, source, me, 1, up_send).start()

        @pl.when(chip > 0)
        def _():
            along(slot, source, me, -1, down_send).start()

        place_own(0, slot)

    def open_whole(slot):
        source = whole_shard(slot)

        @pl.when(chip < chips - 1)
        def _():
            along_whole(slot, source, me, 1, up_whole).start()

        @pl.when(chip > 0)
        def _():
            along_whole(slot, source, me, -1, down_whole).start()

        place_own(1, slot)

    def relay_whole(slot, distance):
        below = me - 2 * distance

        @pl.when(below >= 0)
        def _():
            block = full.at[1, slot, shard_rows(below)]
            along_whole(slot, block, below, 1, up_whole).wait_recv()

            @pl.when(chip < chips - 1)
            def _():
                along_whole(slot, block, below, 1, up_whole).start()

            whole_to_pair(slot, below).start()

        above = me + 2 * distance

        @pl.when(above < places)
        def _():
            block = full.at[1, slot, shard_rows(above)]
            along_whole(slot, block, above, -1, down_whole).wait_recv()

            @pl.when(chip > 0)
            def _():
                along_whole(slot, block, above, -1, down_whole).start()

            whole_to_pair(slot, above).start()

    def hand_on(turn, slot, owner):
        @pl.when(side == turn)
        def _():
            to_pair(slot, owner, side).start()

        @pl.when(side != turn)
        def _():
            to_mate(slot, owner).start()

    def relay(slot, distance):
        below = me - 2 * distance

        @pl.when(below >= 0)
        def _():
            block = held(0, slot, below, side)
            along(slot, block, below, 1, up_send).wait_recv()

            @pl.when(chip < chips - 1)
            def _():
                along(slot, block, below, 1, up_send).start()

            hand_on(0, slot, below)

        above = me + 2 * distance

        @pl.when(above < places)
        def _():
            block = held(0, slot, above, side)
            along(slot, block, above, -1, down_send).wait_recv()

            @pl.when(chip > 0)
            def _():
                along(slot, block, above, -1, down_send).start()

            hand_on(0, slot, above)

    def bridge(slot, distance):
        for owner in (me - 2 * distance, me + 2 * distance):

            @pl.when(jnp.logical_and(owner >= 0, owner < places))
            def _():
                from_mate(slot, owner).wait_recv()
                to_pair(slot, owner, 1 - side).start()

    def close_slot(slot):
        own_copy(slot).wait()
        shard_to_pair(slot, full.at[side, slot, shard_rows(pair)], pair).wait_recv()

        def from_pair(other, carry):
            @pl.when(other != chip)
            def _():
                owner = 2 * other + 1 - core

                @pl.when(side == 0)
                def _():
                    for which in range(2):
                        to_pair(slot, owner, which).wait_recv()

                @pl.when(side == 1)
                def _():
                    whole_to_pair(slot, owner).wait_recv()

            return carry

        lax.fori_loop(0, chips, from_pair, 0)

    wide = features.shape[1] // HALVES

    def columns(part):
        return pl.ds(part * wide, wide)

    def edge_copy(slot, batch, direction, half_at):
        part = pl.ds(direction * edge, edge)
        return pltpu.make_async_remote_copy(
            src_ref=leaving.at[slot, batch, part, columns(half_at)],
            dst_ref=arrived.at[slot, batch, part, columns(half_at)],
            send_sem=edge_send.at[slot, batch, direction, half_at],
            recv_sem=edge_recv.at[slot, batch, direction, half_at],
            device_id={"graph": me + OFFSETS[direction]},
            device_id_type=MESH,
        )

    def sends(direction):
        there = me + OFFSETS[direction]
        return jnp.logical_and(there >= 0, there < places)

    def receives(direction):
        there = me - OFFSETS[direction]
        return jnp.logical_and(there >= 0, there < places)

    def send_edges(slot, batch, half_at, current):
        leaving[slot, batch, :, columns(half_at)] = jnp.dot(
            select[batch], current, preferred_element_type=jnp.float32
        ).astype(jnp.bfloat16)
        for direction in range(len(OFFSETS)):

            @pl.when(sends(direction))
            def _():
                edge_copy(slot, batch, direction, half_at).start()

    def batch_range(batch):
        return pl.ds(pl.multiple_of(batch * rows, rows), rows)

    def hop(batch, half_at):
        return pltpu.make_async_remote_copy(
            src_ref=out.at[kept - 1, batch_range(batch), columns(half_at)],
            dst_ref=entering.at[batch, :, columns(half_at)],
            send_sem=hop_send.at[batch, half_at],
            recv_sem=hop_recv.at[batch, half_at],
            device_id={"segment": seg + 1},
            device_id_type=MESH,
        )

    def prepare(batch, carry):
        for direction in range(len(OFFSETS)):
            part = pl.ds(direction * edge, edge)
            select[batch, part] = selector(
                send_ids[batch, pl.ds(direction, 1), :], rows
            )
            for slot in range(kept):

                @pl.when(jnp.logical_not(receives(direction)))
                def _():
                    arrived[slot, batch, part] = jnp.zeros(
                        (edge, arrived.shape[3]), jnp.bfloat16
                    )

        initial = features[batch_range(batch), :]

        @pl.when(seg == 0)
        def _():
            entering[batch] = initial

        lookup = selector(hist_ids[pl.ds(batch, 1), :], history.shape[1])
        for slot in range(kept):
            looked = jnp.dot(
                lookup, history[slot], preferred_element_type=jnp.float32
            ).astype(jnp.bfloat16)
            past = transposed_dot(hist_adj[batch], looked)
            base[slot, batch] = (1.0 - ALPHA) * past + ALPHA * initial.astype(jnp.float32)
        return carry

    def layer(slot, batch):
        strength = jnp.float32(0.0)
        for number in range(layer_total):
            value = math.log(LAMBDA / (number + 1.0) + 1.0)
            strength = jnp.where(first_layer + slot == number, jnp.float32(value), strength)
        supports = []
        mixing = [None] * HALVES
        for part in range(HALVES):
            if slot == 0:
                current = entering[batch, :, columns(part)]
            else:
                current = out[slot - 1, batch_range(batch), columns(part)]
            aggregate = jnp.dot(own_adj[batch], current, preferred_element_type=jnp.float32)
            for direction in range(len(OFFSETS)):

                @pl.when(receives(direction))
                def _():
                    edge_copy(slot, batch, direction, part).wait_recv()

            aggregate = aggregate + transposed_dot(
                side_adj[batch], arrived[slot, batch, :, columns(part)]
            )
            support = (1.0 - ALPHA) * aggregate + base[slot, batch, :, columns(part)]
            supports.append(support)
            rounded = support.astype(jnp.bfloat16)
            for target in range(HALVES):
                term = jnp.dot(
                    rounded,
                    full[side, slot, columns(part), columns(target)],
                    preferred_element_type=jnp.float32,
                )
                mixing[target] = term if part == 0 else mixing[target] + term
                if part < HALVES - 1:
                    continue
                mixed = (1.0 - strength) * supports[target] + strength * mixing[target]
                result = jnp.maximum(mixed, 0.0).astype(jnp.bfloat16)
                out[slot, batch_range(batch), columns(target)] = result
                if slot < kept - 1:
                    send_edges(slot + 1, batch, target, result)
                else:

                    @pl.when(seg < segments - 1)
                    def _():
                        hop(batch, target).start()

    far = chips - 1

    def line_steps(slot):
        steps = []
        for distance in range(1, chips):
            work = [(relay, (slot, distance))]
            if distance == max(1, far - 1) and slot < kept - 1:
                work.append((open_slot, (slot + 1,)))
            if distance > 1:
                work.append((bridge, (slot, distance - 1)))
            steps.append(work)
        steps.append([(bridge, (slot, far))])
        return steps

    def run(work):
        for action, arguments in work:
            if action is bridge:

                @pl.when(side == 0)
                def _():
                    action(*arguments)

            else:
                action(*arguments)

    open_slot(0)
    for load in loads:
        load.wait()
    middle = batches // 2
    lax.fori_loop(0, middle, prepare, 0)
    for number, work in enumerate(line_steps(0)):
        if number == far and kept > 1:
            relay(1, 1)
        run(work)
        if number == 0:
            lax.fori_loop(middle, batches, prepare, 0)

            @pl.when(seg == 0)
            def _():
                def early(batch, carry):
                    for part in range(HALVES):
                        send_edges(0, batch, part, entering[batch, :, columns(part)])
                    return carry

                lax.fori_loop(0, batches, early, 0)

    first_tasks = [[] for _ in range(batches * kept)]
    others = []
    for slot in range(1, kept):
        steps = line_steps(slot)
        if slot == 1:
            steps[0] = steps[0][1:]
            steps = [steps[0] + steps[1]] + steps[2:] if far > 1 else steps
        others += steps
        for number, work in enumerate(steps):
            first_tasks[min((slot - 1) * batches + number, slot * batches - 1)] += work

    @pl.when(seg > 0)
    def _():
        for number, work in enumerate(others):
            run(work)
            if number == 0:

                @pl.when(side == 1)
                def _():
                    open_whole(0)

    @pl.when(side == 1)
    def _():
        if not others:
            open_whole(0)
        for slot in range(kept):
            for distance in range(1, chips):
                relay_whole(slot, distance)
                if slot < kept - 1 and distance == max(1, far - 1):
                    open_whole(slot + 1)

    lag = jnp.where(seg == 0, batches, 1)
    ticks = batches + lag * (kept - 1)

    def tick(time, carry):
        @pl.when(jnp.logical_and(seg > 0, time < batches))
        def _():
            for part in range(HALVES):
                hop(time, part).wait_recv()
                send_edges(0, time, part, entering[time, :, columns(part)])

        for number, work in enumerate(first_tasks):
            if work:

                @pl.when(jnp.logical_and(seg == 0, time == number))
                def _():
                    run(work)

        for slot in range(kept - 1, -1, -1):

            @pl.when(time == lag * slot)
            def _():
                close_slot(slot)

            batch = time - lag * slot

            @pl.when(jnp.logical_and(batch >= 0, batch < batches))
            def _():
                layer(slot, batch)

        return carry

    lax.fori_loop(0, ticks, tick, 0)

    def finish(batch, carry):
        for slot in range(kept):
            for direction in range(len(OFFSETS)):

                @pl.when(sends(direction))
                def _():
                    for part in range(HALVES):
                        edge_copy(slot, batch, direction, part).wait_send()

        @pl.when(seg < segments - 1)
        def _():
            for part in range(HALVES):
                hop(batch, part).wait_send()

        return carry

    lax.fori_loop(0, batches, finish, 0)

    def drain(other, carry):
        owner = 2 * other + core
        for slot in range(kept):
            block = held(0, slot, owner, side)

            @pl.when(jnp.logical_and(other <= chip, chip < chips - 1))
            def _():
                along(slot, block, owner, 1, up_send).wait_send()

                @pl.when(side == 1)
                def _():
                    along_whole(slot, whole_shard(slot), owner, 1, up_whole).wait_send()

            @pl.when(jnp.logical_and(other >= chip, chip > 0))
            def _():
                along(slot, block, owner, -1, down_send).wait_send()

                @pl.when(side == 1)
                def _():
                    along_whole(slot, whole_shard(slot), owner, -1, down_whole).wait_send()

            @pl.when(other != chip)
            def _():
                @pl.when(side == 0)
                def _():
                    for which in range(2):
                        to_pair(slot, owner, which).wait_send()

                @pl.when(side == 1)
                def _():
                    to_mate(slot, owner).wait_send()
                    whole_to_pair(slot, owner).wait_send()

            @pl.when(other == chip)
            def _():
                shard_to_pair(slot, whole_shard(slot), owner).wait_send()

        return carry

    lax.fori_loop(0, chips, drain, 0)


def staged(features, weights, history, own_adj, side_adj, hist_adj, send_ids, hist_ids):
    segments = lax.axis_size("segment")
    places = lax.axis_size("graph")
    layer_total, shard, width = weights.shape
    kept = layer_total // segments
    batches, rows = own_adj.shape[0], own_adj.shape[2]
    edges = side_adj.shape[1] * side_adj.shape[2]
    chips = places // 2
    dma = pltpu.SemaphoreType.DMA

    def kernel(*refs):
        stage_kernel(segments, places, layer_total, *refs)

    stored = pl.BlockSpec(memory_space=pl.ANY)
    half = jnp.bfloat16
    return pl.pallas_call(
        kernel,
        out_shape=jax.ShapeDtypeStruct((kept, batches * rows, width), half),
        in_specs=[stored] * 8,
        out_specs=pl.BlockSpec(memory_space=pltpu.VMEM),
        scratch_shapes=[
            pltpu.VMEM(features.shape, half),
            pltpu.VMEM((kept,) + history.shape[1:], half),
            pltpu.VMEM(own_adj.shape, half),
            pltpu.VMEM((batches, edges, rows), half),
            pltpu.VMEM(hist_adj.shape, half),
            pltpu.VMEM(send_ids.shape, send_ids.dtype),
            pltpu.VMEM(hist_ids.shape, hist_ids.dtype),
            pltpu.VMEM((2, kept, places * shard, width), half),
            pltpu.VMEM((kept, batches, rows, width), jnp.float32),
            pltpu.VMEM((batches, edges, rows), half),
            pltpu.VMEM((batches, rows, width), half),
            pltpu.VMEM((kept, batches, edges, width), half),
            pltpu.VMEM((kept, batches, edges, width), half),
            dma((7,)),
            dma((kept,)),
            dma((2, kept, chips)),
            dma((kept, chips)),
            dma((kept, 2, chips)),
            dma((kept,)),
            dma((kept, chips)),
            dma((kept, chips)),
            dma((kept, chips)),
            dma((kept, chips)),
            dma((kept, chips)),
            dma((kept, 2, chips)),
            dma((kept,)),
            dma((kept, batches, len(OFFSETS), HALVES)),
            dma((kept, batches, len(OFFSETS), HALVES)),
            dma((batches, HALVES)),
            dma((batches, HALVES)),
        ],
        compiler_params=pltpu.CompilerParams(
            collective_id=0, has_side_effects=True, vmem_limit_bytes=60 * 1024 * 1024
        ),
    )(
        features,
        weights,
        history,
        own_adj,
        side_adj.reshape(batches, edges, rows),
        hist_adj,
        send_ids,
        hist_ids,
    )


def device_part(features, weights, *rest):
    places, segments = lax.axis_size("graph"), lax.axis_size("segment")
    whole_tiles = weights.shape[1] % (2 * TILE_ROWS) == 0 and rest[2].shape[2] % TILE_ROWS == 0
    even = places % 2 == 0 and segments % 2 == 0 and weights.shape[0] % segments == 0
    whole_tiles = whole_tiles and features.shape[1] % (HALVES * TILE_COLUMNS) == 0
    if whole_tiles and even:
        return staged(features, weights, *rest)
    return shards(features, weights, *rest)


def solution(mesh):
    in_specs = (
        P("graph", None),
        P(None, "graph", None),
        P(None, "graph", None),
        P(None, "graph", None),
        P(None, None, "graph", None),
        P(None, "graph", None),
        P(None, None, "graph"),
        P(None, "graph"),
    )
    out_specs = P("segment", "graph", None)
    return jax.shard_map(device_part, mesh=mesh, in_specs=in_specs, out_specs=out_specs, check_vma=False)
```

```python
import math

import jax
import jax.numpy as jnp
from jax import lax
from jax.experimental import pallas as pl
from jax.experimental.pallas import tpu as pltpu
from jax.sharding import PartitionSpec as P

ALPHA = 0.1
LAMBDA = 1.5
OFFSETS = (1, -1, 2, -2)


def shifted(value, axis, steps):
    count = lax.axis_size(axis)
    initial, last = (max(0, -steps), min(count, count - steps))
    return lax.ppermute(value, axis, [(source, source + steps) for source in range(initial, last)])


def propagate(
    current, initial, layer_number, weight, tables, own_tile, side_tile, send_rows, past_rows
):
    edge_count = send_rows.shape[1]
    picked = jnp.take(current, send_rows.reshape(-1), axis=0)
    arrived = []
    for direction in range(len(OFFSETS)):
        outgoing = picked[direction * edge_count : (direction + 1) * edge_count]
        arrived.append(shifted(outgoing, "graph", OFFSETS[direction]))
    layer_table = lax.dynamic_index_in_dim(tables, layer_number, 0, keepdims=False)
    arrived.append(jnp.take(layer_table, past_rows, axis=0))
    gathered_rows = jnp.concatenate(arrived, axis=0)
    aggregate = jnp.dot(own_tile, current, preferred_element_type=jnp.float32)
    aggregate = aggregate + lax.dot_general(
        side_tile, gathered_rows, (((0,), (0,)), ((), ())), preferred_element_type=jnp.float32
    )
    support = (1.0 - ALPHA) * aggregate + ALPHA * initial.astype(jnp.float32)
    mixing = jnp.dot(support.astype(jnp.bfloat16), weight, preferred_element_type=jnp.float32)
    strength = jnp.log(LAMBDA / (layer_number.astype(jnp.float32) + 1.0) + 1.0)
    return jax.nn.relu((1.0 - strength) * support + strength * mixing).astype(jnp.bfloat16)


def batch_tiles(own_adj, side_adj, hist_adj, send_ids, hist_ids, batch_safe):
    batch_rows = own_adj.shape[2]
    side_edges = side_adj.shape[1] * side_adj.shape[2]
    own_tile = lax.dynamic_index_in_dim(own_adj, batch_safe, 0, keepdims=False)
    edge_tile = lax.dynamic_index_in_dim(side_adj, batch_safe, 0, keepdims=False).reshape(
        side_edges, batch_rows
    )
    past_tile = lax.dynamic_index_in_dim(hist_adj, batch_safe, 0, keepdims=False)
    side_tile = jnp.concatenate([edge_tile, past_tile], axis=0)
    send_rows = lax.dynamic_index_in_dim(send_ids, batch_safe, 0, keepdims=False)
    past_rows = lax.dynamic_index_in_dim(hist_ids, batch_safe, 0, keepdims=False)
    return (own_tile, side_tile, send_rows, past_rows)


def shards(features, weights, history, own_adj, side_adj, hist_adj, send_ids, hist_ids):
    segment_pos = lax.axis_index("segment")
    segment_count = lax.axis_size("segment")
    batch_count = own_adj.shape[0]
    batch_rows = own_adj.shape[2]
    layer_total = weights.shape[0]
    kept_slots = layer_total // segment_count
    initial = lax.dynamic_slice_in_dim(features, segment_pos * batch_rows, batch_rows, 0)
    own_tile, side_tile, send_rows, past_rows = batch_tiles(
        own_adj, side_adj, hist_adj, send_ids, hist_ids, segment_pos
    )
    current = initial
    produced = []
    for number in range(layer_total):
        weight = lax.all_gather(weights[number], "graph", axis=0, tiled=True)
        current = propagate(
            current,
            initial,
            jnp.int32(number),
            weight,
            history,
            own_tile,
            side_tile,
            send_rows,
            past_rows,
        )
        produced.append(current)
    arranged = jnp.stack(
        [
            jnp.stack([produced[kept_slots * target + slot] for target in range(segment_count)])
            for slot in range(kept_slots)
        ]
    )
    received = lax.all_to_all(arranged, "segment", split_axis=1, concat_axis=1, tiled=True)
    return received.reshape(kept_slots, batch_count * batch_rows, features.shape[1])


TILE_ROWS = 16
MESH = pl.DeviceIdType.MESH


def column_of(row):
    count = row.shape[1]
    down = lax.broadcasted_iota(jnp.int32, (count, count), 0)
    across = lax.broadcasted_iota(jnp.int32, (count, count), 1)
    spread = jnp.broadcast_to(row.astype(jnp.float32), (count, count))
    return jnp.sum(jnp.where(down == across, spread, 0.0), axis=1, keepdims=True)


def selector(row, width):
    across = lax.broadcasted_iota(jnp.int32, (row.shape[1], width), 1).astype(jnp.float32)
    return jnp.where(across == column_of(row), 1.0, 0.0).astype(jnp.bfloat16)


def transposed_dot(left, right):
    return lax.dot_general(
        left, right, (((0,), (0,)), ((), ())), preferred_element_type=jnp.float32
    )


def stage_kernel(
    segments, places, layer_total,
    features_in, weights, history_in, own_in, side_in, hist_in, send_in, ids_in,
    out,
    features, history, own_adj, side_adj, hist_adj, send_ids, hist_ids,
    full, base, select, crossed, entering, leaving, arrived,
    load_sem, own_sem, line_recv, mate_recv, pair_recv, shard_recv,
    up_send, down_send, up_whole, down_whole, mate_send, pair_send, shard_send,
    edge_send, edge_recv, hop_send, hop_recv,
):
    seg = lax.axis_index("segment")
    me = lax.axis_index("graph")
    kept = layer_total // segments
    batches, rows = own_adj.shape[0], own_adj.shape[2]
    shard = weights.shape[1]
    piece = shard // 2
    edge = send_ids.shape[2]
    chips = places // 2
    chip = me // 2
    core = me % 2
    pair = me + 1 - 2 * core
    half = segments // 2
    side = seg // half
    mate = seg + half - 2 * half * side
    first_layer = seg * kept

    loads = [
        pltpu.make_async_copy(source, target, load_sem.at[number])
        for number, (source, target) in enumerate(
            [
                (features_in, features),
                (history_in.at[pl.ds(first_layer, kept)], history),
                (own_in, own_adj),
                (side_in, side_adj),
                (hist_in, hist_adj),
                (send_in, send_ids),
                (ids_in, hist_ids),
            ]
        )
    ]
    for load in loads:
        load.start()

    barrier = pltpu.get_barrier_semaphore()
    expected = jnp.int32(1)
    pl.semaphore_signal(barrier, inc=1, device_id={"segment": mate}, device_id_type=MESH)
    for offset in OFFSETS:
        there = me + offset
        inside = jnp.logical_and(there >= 0, there < places)

        @pl.when(inside)
        def _():
            pl.semaphore_signal(barrier, inc=1, device_id={"graph": there}, device_id_type=MESH)

        expected = expected + inside.astype(jnp.int32)
    for step in (1, -1):
        beside = seg + step
        inside = jnp.logical_and(beside >= 0, beside < segments)

        @pl.when(inside)
        def _():
            pl.semaphore_signal(
                barrier, inc=1, device_id={"segment": beside}, device_id_type=MESH
            )

        expected = expected + inside.astype(jnp.int32)
    pl.semaphore_wait(barrier, expected)


    def shard_rows(owner):
        return pl.ds(pl.multiple_of(owner * shard, shard), shard)

    def piece_rows(owner, which):
        return pl.ds(pl.multiple_of(owner * shard + which * piece, piece), piece)

    def whole_shard(slot):
        return weights.at[first_layer + slot]

    def own_copy(slot):
        return pltpu.make_async_copy(
            whole_shard(slot), full.at[side, slot, shard_rows(me)], own_sem.at[slot]
        )

    def push(turn, slot, source, owner, which, target, send_sem, recv_sem):
        return pltpu.make_async_remote_copy(
            src_ref=source,
            dst_ref=full.at[turn, slot, piece_rows(owner, which)],
            send_sem=send_sem,
            recv_sem=recv_sem,
            device_id=target,
            device_id_type=MESH,
        )

    def held(turn, slot, owner, which):
        return full.at[turn, slot, piece_rows(owner, which)]

    def along(slot, source, owner, step, send_sem):
        return push(
            0, slot, source, owner, side, {"graph": me + 2 * step},
            send_sem.at[slot, owner // 2], line_recv.at[0, slot, owner // 2],
        )

    def along_whole(slot, source, owner, step, send_sem):
        return pltpu.make_async_remote_copy(
            src_ref=source,
            dst_ref=full.at[1, slot, shard_rows(owner)],
            send_sem=send_sem.at[slot, owner // 2],
            recv_sem=line_recv.at[1, slot, owner // 2],
            device_id={"graph": me + 2 * step},
            device_id_type=MESH,
        )

    def whole_to_pair(slot, owner):
        block = full.at[1, slot, shard_rows(owner)]
        return pltpu.make_async_remote_copy(
            src_ref=block,
            dst_ref=block,
            send_sem=pair_send.at[slot, 0, owner // 2],
            recv_sem=pair_recv.at[slot, 0, owner // 2],
            device_id={"graph": pair},
            device_id_type=MESH,
        )

    def to_pair(slot, owner, which):
        return push(
            side, slot, held(side, slot, owner, which), owner, which, {"graph": pair},
            pair_send.at[slot, which, owner // 2], pair_recv.at[slot, which, owner // 2],
        )

    def to_mate(slot, owner):
        turn = 1 - side
        return push(
            turn, slot, held(turn, slot, owner, side), owner, side, {"segment": mate},
            mate_send.at[slot, owner // 2], mate_recv.at[slot, owner // 2],
        )

    def from_mate(slot, owner):
        which = 1 - side
        return push(
            side, slot, held(side, slot, owner, which), owner, which, {"segment": mate},
            mate_send.at[slot, owner // 2], mate_recv.at[slot, owner // 2],
        )

    def shard_to_pair(slot, source, owner):
        return pltpu.make_async_remote_copy(
            src_ref=source,
            dst_ref=full.at[side, slot, shard_rows(owner)],
            send_sem=shard_send.at[slot],
            recv_sem=shard_recv.at[slot],
            device_id={"graph": pair},
            device_id_type=MESH,
        )

    def half_shard(turn, slot):
        number = (seg + (turn - side) * half) * kept + slot
        return weights.at[number, pl.ds(pl.multiple_of(side * piece, piece), piece)]

    def place_own(turn, slot):
        @pl.when(side == turn)
        def _():
            shard_to_pair(slot, whole_shard(slot), me).start()
            own_copy(slot).start()

    def open_slot(slot):
        source = half_shard(0, slot)

        @pl.when(chip < chips - 1)
        def _():
            along(slot, source, me, 1, up_send).start()

        @pl.when(chip > 0)
        def _():
            along(slot, source, me, -1, down_send).start()

        place_own(0, slot)

    def open_whole(slot):
        source = whole_shard(slot)

        @pl.when(chip < chips - 1)
        def _():
            along_whole(slot, source, me, 1, up_whole).start()

        @pl.when(chip > 0)
        def _():
            along_whole(slot, source, me, -1, down_whole).start()

        place_own(1, slot)

    def relay_whole(slot, distance):
        below = me - 2 * distance

        @pl.when(below >= 0)
        def _():
            block = full.at[1, slot, shard_rows(below)]
            along_whole(slot, block, below, 1, up_whole).wait_recv()

            @pl.when(chip < chips - 1)
            def _():
                along_whole(slot, block, below, 1, up_whole).start()

            whole_to_pair(slot, below).start()

        above = me + 2 * distance

        @pl.when(above < places)
        def _():
            block = full.at[1, slot, shard_rows(above)]
            along_whole(slot, block, above, -1, down_whole).wait_recv()

            @pl.when(chip > 0)
            def _():
                along_whole(slot, block, above, -1, down_whole).start()

            whole_to_pair(slot, above).start()

    def hand_on(turn, slot, owner):
        @pl.when(side == turn)
        def _():
            to_pair(slot, owner, side).start()

        @pl.when(side != turn)
        def _():
            to_mate(slot, owner).start()

    def relay(slot, distance):
        below = me - 2 * distance

        @pl.when(below >= 0)
        def _():
            block = held(0, slot, below, side)
            along(slot, block, below, 1, up_send).wait_recv()

            @pl.when(chip < chips - 1)
            def _():
                along(slot, block, below, 1, up_send).start()

            hand_on(0, slot, below)

        above = me + 2 * distance

        @pl.when(above < places)
        def _():
            block = held(0, slot, above, side)
            along(slot, block, above, -1, down_send).wait_recv()

            @pl.when(chip > 0)
            def _():
                along(slot, block, above, -1, down_send).start()

            hand_on(0, slot, above)

    def bridge(slot, distance):
        for owner in (me - 2 * distance, me + 2 * distance):

            @pl.when(jnp.logical_and(owner >= 0, owner < places))
            def _():
                from_mate(slot, owner).wait_recv()
                to_pair(slot, owner, 1 - side).start()

    def close_slot(slot):
        own_copy(slot).wait()
        shard_to_pair(slot, full.at[side, slot, shard_rows(pair)], pair).wait_recv()

        def from_pair(other, carry):
            @pl.when(other != chip)
            def _():
                owner = 2 * other + 1 - core

                @pl.when(side == 0)
                def _():
                    for which in range(2):
                        to_pair(slot, owner, which).wait_recv()

                @pl.when(side == 1)
                def _():
                    whole_to_pair(slot, owner).wait_recv()

            return carry

        lax.fori_loop(0, chips, from_pair, 0)

    def edge_copy(slot, batch, direction):
        part = pl.ds(direction * edge, edge)
        return pltpu.make_async_remote_copy(
            src_ref=leaving.at[slot, batch, part],
            dst_ref=arrived.at[slot, batch, part],
            send_sem=edge_send.at[slot, batch, direction],
            recv_sem=edge_recv.at[slot, batch, direction],
            device_id={"graph": me + OFFSETS[direction]},
            device_id_type=MESH,
        )

    def sends(direction):
        there = me + OFFSETS[direction]
        return jnp.logical_and(there >= 0, there < places)

    def receives(direction):
        there = me - OFFSETS[direction]
        return jnp.logical_and(there >= 0, there < places)

    def send_edges(slot, batch, current):
        both = jnp.dot(select[batch], current, preferred_element_type=jnp.float32)
        edges = leaving.shape[2]
        leaving[slot, batch] = both[:edges].astype(jnp.bfloat16)
        for direction in range(len(OFFSETS)):

            @pl.when(sends(direction))
            def _():
                edge_copy(slot, batch, direction).start()

        base[slot, batch] = base[slot, batch] + (1.0 - ALPHA) * both[edges:]

    def batch_range(batch):
        return pl.ds(pl.multiple_of(batch * rows, rows), rows)

    def hop(batch):
        return pltpu.make_async_remote_copy(
            src_ref=out.at[kept - 1, batch_range(batch)],
            dst_ref=entering.at[batch],
            send_sem=hop_send.at[batch],
            recv_sem=hop_recv.at[batch],
            device_id={"segment": seg + 1},
            device_id_type=MESH,
        )

    def prepare(batch, carry):
        for direction in range(len(OFFSETS)):
            part = pl.ds(direction * edge, edge)
            select[batch, part] = selector(
                send_ids[batch, pl.ds(direction, 1), :], rows
            )
            for slot in range(kept):

                @pl.when(jnp.logical_not(receives(direction)))
                def _():
                    arrived[slot, batch, part] = jnp.zeros(
                        (edge, arrived.shape[3]), jnp.bfloat16
                    )

        edges = leaving.shape[2]
        select[batch, pl.ds(edges, rows)] = own_adj[batch]
        crossed[batch] = side_adj[batch].astype(jnp.float32).T.astype(jnp.bfloat16)
        initial = features[batch_range(batch), :]

        @pl.when(seg == 0)
        def _():
            entering[batch] = initial

        lookup = selector(hist_ids[pl.ds(batch, 1), :], history.shape[1])
        for slot in range(kept):
            looked = jnp.dot(
                lookup, history[slot], preferred_element_type=jnp.float32
            ).astype(jnp.bfloat16)
            past = transposed_dot(hist_adj[batch], looked)
            base[slot, batch] = (1.0 - ALPHA) * past + ALPHA * initial.astype(jnp.float32)
        return carry

    def layer(slot, batch):
        strength = jnp.float32(0.0)
        for number in range(layer_total):
            value = math.log(LAMBDA / (number + 1.0) + 1.0)
            strength = jnp.where(first_layer + slot == number, jnp.float32(value), strength)
        for direction in range(len(OFFSETS)):

            @pl.when(receives(direction))
            def _():
                edge_copy(slot, batch, direction).wait_recv()

        received = jnp.dot(
            crossed[batch], arrived[slot, batch], preferred_element_type=jnp.float32
        )
        support = (1.0 - ALPHA) * received + base[slot, batch]
        mixing = jnp.dot(
            support.astype(jnp.bfloat16), full[side, slot], preferred_element_type=jnp.float32
        )
        result = jnp.maximum((1.0 - strength) * support + strength * mixing, 0.0)
        result = result.astype(jnp.bfloat16)
        out[slot, batch_range(batch), :] = result
        if slot < kept - 1:
            send_edges(slot + 1, batch, result)
        else:

            @pl.when(seg < segments - 1)
            def _():
                hop(batch).start()

    far = chips - 1

    def line_steps(slot):
        steps = []
        for distance in range(1, chips):
            work = [(relay, (slot, distance))]
            if distance == max(1, far - 1) and slot < kept - 1:
                work.append((open_slot, (slot + 1,)))
            if distance > 1:
                work.append((bridge, (slot, distance - 1)))
            steps.append(work)
        steps.append([(bridge, (slot, far))])
        return steps

    def run(work):
        for action, arguments in work:
            if action is bridge:

                @pl.when(side == 0)
                def _():
                    action(*arguments)

            else:
                action(*arguments)

    open_slot(0)
    for load in loads:
        load.wait()
    middle = batches // 2
    lax.fori_loop(0, middle, prepare, 0)
    for number, work in enumerate(line_steps(0)):
        if number == far and kept > 1:
            relay(1, 1)
        run(work)
        if number == 0:
            lax.fori_loop(middle, batches, prepare, 0)

            @pl.when(seg == 0)
            def _():
                def early(batch, carry):
                    send_edges(0, batch, entering[batch])
                    return carry

                lax.fori_loop(0, batches, early, 0)

    first_tasks = [[] for _ in range(batches * kept)]
    others = []
    for slot in range(1, kept):
        steps = line_steps(slot)
        if slot == 1:
            steps[0] = steps[0][1:]
            steps = [steps[0] + steps[1]] + steps[2:] if far > 1 else steps
        others += steps
        for number, work in enumerate(steps):
            first_tasks[min((slot - 1) * batches + number, slot * batches - 1)] += work

    @pl.when(seg > 0)
    def _():
        for number, work in enumerate(others):
            run(work)
            if number == 0:

                @pl.when(side == 1)
                def _():
                    open_whole(0)

    @pl.when(side == 1)
    def _():
        if not others:
            open_whole(0)
        for slot in range(kept):
            for distance in range(1, chips):
                relay_whole(slot, distance)
                if slot < kept - 1 and distance == max(1, far - 1):
                    open_whole(slot + 1)

    lag = jnp.where(seg == 0, batches, 1)
    ticks = batches + lag * (kept - 1)

    def tick(time, carry):
        @pl.when(jnp.logical_and(seg > 0, time < batches))
        def _():
            hop(time).wait_recv()
            send_edges(0, time, entering[time])

        for number, work in enumerate(first_tasks):
            if work:

                @pl.when(jnp.logical_and(seg == 0, time == number))
                def _():
                    run(work)

        for slot in range(kept - 1, -1, -1):

            @pl.when(time == lag * slot)
            def _():
                close_slot(slot)

            batch = time - lag * slot

            @pl.when(jnp.logical_and(batch >= 0, batch < batches))
            def _():
                layer(slot, batch)

        return carry

    lax.fori_loop(0, ticks, tick, 0)

    def finish(batch, carry):
        for slot in range(kept):
            for direction in range(len(OFFSETS)):

                @pl.when(sends(direction))
                def _():
                    edge_copy(slot, batch, direction).wait_send()

        @pl.when(seg < segments - 1)
        def _():
            hop(batch).wait_send()

        return carry

    lax.fori_loop(0, batches, finish, 0)

    def drain(other, carry):
        owner = 2 * other + core
        for slot in range(kept):
            block = held(0, slot, owner, side)

            @pl.when(jnp.logical_and(other <= chip, chip < chips - 1))
            def _():
                along(slot, block, owner, 1, up_send).wait_send()

                @pl.when(side == 1)
                def _():
                    along_whole(slot, whole_shard(slot), owner, 1, up_whole).wait_send()

            @pl.when(jnp.logical_and(other >= chip, chip > 0))
            def _():
                along(slot, block, owner, -1, down_send).wait_send()

                @pl.when(side == 1)
                def _():
                    along_whole(slot, whole_shard(slot), owner, -1, down_whole).wait_send()

            @pl.when(other != chip)
            def _():
                @pl.when(side == 0)
                def _():
                    for which in range(2):
                        to_pair(slot, owner, which).wait_send()

                @pl.when(side == 1)
                def _():
                    to_mate(slot, owner).wait_send()
                    whole_to_pair(slot, owner).wait_send()

            @pl.when(other == chip)
            def _():
                shard_to_pair(slot, whole_shard(slot), owner).wait_send()

        return carry

    lax.fori_loop(0, chips, drain, 0)


def staged(features, weights, history, own_adj, side_adj, hist_adj, send_ids, hist_ids):
    segments = lax.axis_size("segment")
    places = lax.axis_size("graph")
    layer_total, shard, width = weights.shape
    kept = layer_total // segments
    batches, rows = own_adj.shape[0], own_adj.shape[2]
    edges = side_adj.shape[1] * side_adj.shape[2]
    chips = places // 2
    dma = pltpu.SemaphoreType.DMA

    def kernel(*refs):
        stage_kernel(segments, places, layer_total, *refs)

    anywhere = pl.BlockSpec(memory_space=pl.ANY)
    half = jnp.bfloat16
    return pl.pallas_call(
        kernel,
        out_shape=jax.ShapeDtypeStruct((kept, batches * rows, width), half),
        in_specs=[anywhere] * 8,
        out_specs=pl.BlockSpec(memory_space=pltpu.VMEM),
        scratch_shapes=[
            pltpu.VMEM(features.shape, half),
            pltpu.VMEM((kept,) + history.shape[1:], half),
            pltpu.VMEM(own_adj.shape, half),
            pltpu.VMEM((batches, edges, rows), half),
            pltpu.VMEM(hist_adj.shape, half),
            pltpu.VMEM(send_ids.shape, send_ids.dtype),
            pltpu.VMEM(hist_ids.shape, hist_ids.dtype),
            pltpu.VMEM((2, kept, places * shard, width), half),
            pltpu.VMEM((kept, batches, rows, width), jnp.float32),
            pltpu.VMEM((batches, edges + rows, rows), half),
            pltpu.VMEM((batches, rows, edges), half),
            pltpu.VMEM((batches, rows, width), half),
            pltpu.VMEM((kept, batches, edges, width), half),
            pltpu.VMEM((kept, batches, edges, width), half),
            dma((7,)),
            dma((kept,)),
            dma((2, kept, chips)),
            dma((kept, chips)),
            dma((kept, 2, chips)),
            dma((kept,)),
            dma((kept, chips)),
            dma((kept, chips)),
            dma((kept, chips)),
            dma((kept, chips)),
            dma((kept, chips)),
            dma((kept, 2, chips)),
            dma((kept,)),
            dma((kept, batches, len(OFFSETS))),
            dma((kept, batches, len(OFFSETS))),
            dma((batches,)),
            dma((batches,)),
        ],
        compiler_params=pltpu.CompilerParams(
            collective_id=0, has_side_effects=True, vmem_limit_bytes=60 * 1024 * 1024
        ),
    )(
        features,
        weights,
        history,
        own_adj,
        side_adj.reshape(batches, edges, rows),
        hist_adj,
        send_ids,
        hist_ids,
    )


def device_part(features, weights, *rest):
    places, segments = lax.axis_size("graph"), lax.axis_size("segment")
    whole_tiles = weights.shape[1] % (2 * TILE_ROWS) == 0 and rest[2].shape[2] % TILE_ROWS == 0
    even = places % 2 == 0 and segments % 2 == 0 and weights.shape[0] % segments == 0
    if whole_tiles and even:
        return staged(features, weights, *rest)
    return shards(features, weights, *rest)


def solution(mesh):
    in_specs = (
        P("graph", None),
        P(None, "graph", None),
        P(None, "graph", None),
        P(None, "graph", None),
        P(None, None, "graph", None),
        P(None, "graph", None),
        P(None, None, "graph"),
        P(None, "graph"),
    )
    out_specs = P("segment", "graph", None)
    return jax.shard_map(device_part, mesh=mesh, in_specs=in_specs, out_specs=out_specs, check_vma=False)
```

```python
import math

import jax
import jax.numpy as jnp
from jax import lax
from jax.experimental import pallas as pl
from jax.experimental.pallas import tpu as pltpu
from jax.sharding import PartitionSpec as P

ALPHA = 0.1
LAMBDA = 1.5
OFFSETS = (1, -1, 2, -2)


def shifted(value, axis, steps):
    count = lax.axis_size(axis)
    initial, last = (max(0, -steps), min(count, count - steps))
    return lax.ppermute(value, axis, [(source, source + steps) for source in range(initial, last)])


def propagate(
    current, initial, layer_number, weight, tables, own_tile, side_tile, send_rows, past_rows
):
    edge_count = send_rows.shape[1]
    picked = jnp.take(current, send_rows.reshape(-1), axis=0)
    arrived = []
    for direction in range(len(OFFSETS)):
        outgoing = picked[direction * edge_count : (direction + 1) * edge_count]
        arrived.append(shifted(outgoing, "graph", OFFSETS[direction]))
    layer_table = lax.dynamic_index_in_dim(tables, layer_number, 0, keepdims=False)
    arrived.append(jnp.take(layer_table, past_rows, axis=0))
    gathered_rows = jnp.concatenate(arrived, axis=0)
    aggregate = jnp.dot(own_tile, current, preferred_element_type=jnp.float32)
    aggregate = aggregate + lax.dot_general(
        side_tile, gathered_rows, (((0,), (0,)), ((), ())), preferred_element_type=jnp.float32
    )
    support = (1.0 - ALPHA) * aggregate + ALPHA * initial.astype(jnp.float32)
    mixing = jnp.dot(support.astype(jnp.bfloat16), weight, preferred_element_type=jnp.float32)
    strength = jnp.log(LAMBDA / (layer_number.astype(jnp.float32) + 1.0) + 1.0)
    return jax.nn.relu((1.0 - strength) * support + strength * mixing).astype(jnp.bfloat16)


def batch_tiles(own_adj, side_adj, hist_adj, send_ids, hist_ids, batch_safe):
    batch_rows = own_adj.shape[2]
    side_edges = side_adj.shape[1] * side_adj.shape[2]
    own_tile = lax.dynamic_index_in_dim(own_adj, batch_safe, 0, keepdims=False)
    edge_tile = lax.dynamic_index_in_dim(side_adj, batch_safe, 0, keepdims=False).reshape(
        side_edges, batch_rows
    )
    past_tile = lax.dynamic_index_in_dim(hist_adj, batch_safe, 0, keepdims=False)
    side_tile = jnp.concatenate([edge_tile, past_tile], axis=0)
    send_rows = lax.dynamic_index_in_dim(send_ids, batch_safe, 0, keepdims=False)
    past_rows = lax.dynamic_index_in_dim(hist_ids, batch_safe, 0, keepdims=False)
    return (own_tile, side_tile, send_rows, past_rows)


def shards(features, weights, history, own_adj, side_adj, hist_adj, send_ids, hist_ids):
    segment_pos = lax.axis_index("segment")
    segment_count = lax.axis_size("segment")
    batch_count = own_adj.shape[0]
    batch_rows = own_adj.shape[2]
    layer_total = weights.shape[0]
    kept_slots = layer_total // segment_count
    initial = lax.dynamic_slice_in_dim(features, segment_pos * batch_rows, batch_rows, 0)
    own_tile, side_tile, send_rows, past_rows = batch_tiles(
        own_adj, side_adj, hist_adj, send_ids, hist_ids, segment_pos
    )
    current = initial
    produced = []
    for number in range(layer_total):
        weight = lax.all_gather(weights[number], "graph", axis=0, tiled=True)
        current = propagate(
            current,
            initial,
            jnp.int32(number),
            weight,
            history,
            own_tile,
            side_tile,
            send_rows,
            past_rows,
        )
        produced.append(current)
    arranged = jnp.stack(
        [
            jnp.stack([produced[kept_slots * target + slot] for target in range(segment_count)])
            for slot in range(kept_slots)
        ]
    )
    received = lax.all_to_all(arranged, "segment", split_axis=1, concat_axis=1, tiled=True)
    return received.reshape(kept_slots, batch_count * batch_rows, features.shape[1])


TILE_ROWS = 16
MESH = pl.DeviceIdType.MESH


def column_of(row):
    count = row.shape[1]
    down = lax.broadcasted_iota(jnp.int32, (count, count), 0)
    across = lax.broadcasted_iota(jnp.int32, (count, count), 1)
    spread = jnp.broadcast_to(row.astype(jnp.float32), (count, count))
    return jnp.sum(jnp.where(down == across, spread, 0.0), axis=1, keepdims=True)


def selector(row, width):
    across = lax.broadcasted_iota(jnp.int32, (row.shape[1], width), 1).astype(jnp.float32)
    return jnp.where(across == column_of(row), 1.0, 0.0).astype(jnp.bfloat16)


def transposed_dot(left, right):
    return lax.dot_general(
        left, right, (((0,), (0,)), ((), ())), preferred_element_type=jnp.float32
    )


def stage_kernel(
    segments, places, layer_total,
    features_in, weights, history_in, own_in, side_in, hist_in, send_in, ids_in,
    out,
    features, history, own_adj, side_adj, hist_adj, send_ids, hist_ids,
    made, full, base, select, crossed, entering, leaving, arrived,
    load_sem, own_sem, store_sem, line_recv, mate_recv, pair_recv, shard_recv,
    up_send, down_send, up_whole, down_whole, mate_send, pair_send, shard_send,
    edge_send, edge_recv, hop_send, hop_recv,
):
    seg = lax.axis_index("segment")
    me = lax.axis_index("graph")
    kept = layer_total // segments
    batches, rows = own_adj.shape[0], own_adj.shape[2]
    shard = weights.shape[1]
    piece = shard // 2
    edge = send_ids.shape[2]
    chips = places // 2
    chip = me // 2
    core = me % 2
    pair = me + 1 - 2 * core
    half = segments // 2
    side = seg // half
    mate = seg + half - 2 * half * side
    first_layer = seg * kept

    loads = [
        pltpu.make_async_copy(source, target, load_sem.at[number])
        for number, (source, target) in enumerate(
            [
                (features_in, features),
                (history_in.at[pl.ds(first_layer, kept)], history),
                (own_in, own_adj),
                (side_in, side_adj),
                (hist_in, hist_adj),
                (send_in, send_ids),
                (ids_in, hist_ids),
            ]
        )
    ]
    for load in loads:
        load.start()

    barrier = pltpu.get_barrier_semaphore()
    expected = jnp.int32(1)
    pl.semaphore_signal(barrier, inc=1, device_id={"segment": mate}, device_id_type=MESH)
    for offset in OFFSETS:
        there = me + offset
        inside = jnp.logical_and(there >= 0, there < places)

        @pl.when(inside)
        def _():
            pl.semaphore_signal(barrier, inc=1, device_id={"graph": there}, device_id_type=MESH)

        expected = expected + inside.astype(jnp.int32)
    for step in (1, -1):
        beside = seg + step
        inside = jnp.logical_and(beside >= 0, beside < segments)

        @pl.when(inside)
        def _():
            pl.semaphore_signal(
                barrier, inc=1, device_id={"segment": beside}, device_id_type=MESH
            )

        expected = expected + inside.astype(jnp.int32)
    pl.semaphore_wait(barrier, expected)


    def shard_rows(owner):
        return pl.ds(pl.multiple_of(owner * shard, shard), shard)

    def piece_rows(owner, which):
        return pl.ds(pl.multiple_of(owner * shard + which * piece, piece), piece)

    def whole_shard(slot):
        return weights.at[first_layer + slot]

    def own_copy(slot):
        return pltpu.make_async_copy(
            whole_shard(slot), full.at[side, slot, shard_rows(me)], own_sem.at[slot]
        )

    def push(turn, slot, source, owner, which, target, send_sem, recv_sem):
        return pltpu.make_async_remote_copy(
            src_ref=source,
            dst_ref=full.at[turn, slot, piece_rows(owner, which)],
            send_sem=send_sem,
            recv_sem=recv_sem,
            device_id=target,
            device_id_type=MESH,
        )

    def held(turn, slot, owner, which):
        return full.at[turn, slot, piece_rows(owner, which)]

    def along(slot, source, owner, step, send_sem):
        return push(
            0, slot, source, owner, side, {"graph": me + 2 * step},
            send_sem.at[slot, owner // 2], line_recv.at[0, slot, owner // 2],
        )

    def along_whole(slot, source, owner, step, send_sem):
        return pltpu.make_async_remote_copy(
            src_ref=source,
            dst_ref=full.at[1, slot, shard_rows(owner)],
            send_sem=send_sem.at[slot, owner // 2],
            recv_sem=line_recv.at[1, slot, owner // 2],
            device_id={"graph": me + 2 * step},
            device_id_type=MESH,
        )

    def whole_to_pair(slot, owner):
        block = full.at[1, slot, shard_rows(owner)]
        return pltpu.make_async_remote_copy(
            src_ref=block,
            dst_ref=block,
            send_sem=pair_send.at[slot, 0, owner // 2],
            recv_sem=pair_recv.at[slot, 0, owner // 2],
            device_id={"graph": pair},
            device_id_type=MESH,
        )

    def to_pair(slot, owner, which):
        return push(
            side, slot, held(side, slot, owner, which), owner, which, {"graph": pair},
            pair_send.at[slot, which, owner // 2], pair_recv.at[slot, which, owner // 2],
        )

    def to_mate(slot, owner):
        turn = 1 - side
        return push(
            turn, slot, held(turn, slot, owner, side), owner, side, {"segment": mate},
            mate_send.at[slot, owner // 2], mate_recv.at[slot, owner // 2],
        )

    def from_mate(slot, owner):
        which = 1 - side
        return push(
            side, slot, held(side, slot, owner, which), owner, which, {"segment": mate},
            mate_send.at[slot, owner // 2], mate_recv.at[slot, owner // 2],
        )

    def shard_to_pair(slot, source, owner):
        return pltpu.make_async_remote_copy(
            src_ref=source,
            dst_ref=full.at[side, slot, shard_rows(owner)],
            send_sem=shard_send.at[slot],
            recv_sem=shard_recv.at[slot],
            device_id={"graph": pair},
            device_id_type=MESH,
        )

    def half_shard(turn, slot):
        number = (seg + (turn - side) * half) * kept + slot
        return weights.at[number, pl.ds(pl.multiple_of(side * piece, piece), piece)]

    def place_own(turn, slot):
        @pl.when(side == turn)
        def _():
            shard_to_pair(slot, whole_shard(slot), me).start()
            own_copy(slot).start()

    def open_slot(slot):
        source = half_shard(0, slot)

        @pl.when(chip < chips - 1)
        def _():
            along(slot, source, me, 1, up_send).start()

        @pl.when(chip > 0)
        def _():
            along(slot, source, me, -1, down_send).start()

        place_own(0, slot)

    def open_whole(slot):
        source = whole_shard(slot)

        @pl.when(chip < chips - 1)
        def _():
            along_whole(slot, source, me, 1, up_whole).start()

        @pl.when(chip > 0)
        def _():
            along_whole(slot, source, me, -1, down_whole).start()

        place_own(1, slot)

    def relay_whole(slot, distance):
        below = me - 2 * distance

        @pl.when(below >= 0)
        def _():
            block = full.at[1, slot, shard_rows(below)]
            along_whole(slot, block, below, 1, up_whole).wait_recv()

            @pl.when(chip < chips - 1)
            def _():
                along_whole(slot, block, below, 1, up_whole).start()

            whole_to_pair(slot, below).start()

        above = me + 2 * distance

        @pl.when(above < places)
        def _():
            block = full.at[1, slot, shard_rows(above)]
            along_whole(slot, block, above, -1, down_whole).wait_recv()

            @pl.when(chip > 0)
            def _():
                along_whole(slot, block, above, -1, down_whole).start()

            whole_to_pair(slot, above).start()

    def hand_on(turn, slot, owner):
        @pl.when(side == turn)
        def _():
            to_pair(slot, owner, side).start()

        @pl.when(side != turn)
        def _():
            to_mate(slot, owner).start()

    def relay(slot, distance):
        below = me - 2 * distance

        @pl.when(below >= 0)
        def _():
            block = held(0, slot, below, side)
            along(slot, block, below, 1, up_send).wait_recv()

            @pl.when(chip < chips - 1)
            def _():
                along(slot, block, below, 1, up_send).start()

            hand_on(0, slot, below)

        above = me + 2 * distance

        @pl.when(above < places)
        def _():
            block = held(0, slot, above, side)
            along(slot, block, above, -1, down_send).wait_recv()

            @pl.when(chip > 0)
            def _():
                along(slot, block, above, -1, down_send).start()

            hand_on(0, slot, above)

    def bridge(slot, distance):
        for owner in (me - 2 * distance, me + 2 * distance):

            @pl.when(jnp.logical_and(owner >= 0, owner < places))
            def _():
                from_mate(slot, owner).wait_recv()
                to_pair(slot, owner, 1 - side).start()

    def close_slot(slot):
        own_copy(slot).wait()
        shard_to_pair(slot, full.at[side, slot, shard_rows(pair)], pair).wait_recv()

        def from_pair(other, carry):
            @pl.when(other != chip)
            def _():
                owner = 2 * other + 1 - core

                @pl.when(side == 0)
                def _():
                    for which in range(2):
                        to_pair(slot, owner, which).wait_recv()

                @pl.when(side == 1)
                def _():
                    whole_to_pair(slot, owner).wait_recv()

            return carry

        lax.fori_loop(0, chips, from_pair, 0)

    def edge_copy(slot, batch, direction):
        part = pl.ds(direction * edge, edge)
        return pltpu.make_async_remote_copy(
            src_ref=leaving.at[slot, batch, part],
            dst_ref=arrived.at[slot, batch, part],
            send_sem=edge_send.at[slot, batch, direction],
            recv_sem=edge_recv.at[slot, batch, direction],
            device_id={"graph": me + OFFSETS[direction]},
            device_id_type=MESH,
        )

    def sends(direction):
        there = me + OFFSETS[direction]
        return jnp.logical_and(there >= 0, there < places)

    def receives(direction):
        there = me - OFFSETS[direction]
        return jnp.logical_and(there >= 0, there < places)

    def send_edges(slot, batch, current):
        both = jnp.dot(select[batch], current, preferred_element_type=jnp.float32)
        edges = leaving.shape[2]
        leaving[slot, batch] = both[:edges].astype(jnp.bfloat16)
        for direction in range(len(OFFSETS)):

            @pl.when(sends(direction))
            def _():
                edge_copy(slot, batch, direction).start()

        base[slot, batch] = base[slot, batch] + (1.0 - ALPHA) * both[edges:]

    def batch_range(batch):
        return pl.ds(pl.multiple_of(batch * rows, rows), rows)

    def store(slot, batch):
        return pltpu.make_async_copy(
            made.at[slot, batch_range(batch)],
            out.at[slot, batch_range(batch)],
            store_sem.at[slot, batch],
        )

    def hop(batch):
        return pltpu.make_async_remote_copy(
            src_ref=made.at[kept - 1, batch_range(batch)],
            dst_ref=entering.at[batch],
            send_sem=hop_send.at[batch],
            recv_sem=hop_recv.at[batch],
            device_id={"segment": seg + 1},
            device_id_type=MESH,
        )

    def prepare(batch, carry):
        for direction in range(len(OFFSETS)):
            part = pl.ds(direction * edge, edge)
            select[batch, part] = selector(
                send_ids[batch, pl.ds(direction, 1), :], rows
            )
            for slot in range(kept):

                @pl.when(jnp.logical_not(receives(direction)))
                def _():
                    arrived[slot, batch, part] = jnp.zeros(
                        (edge, arrived.shape[3]), jnp.bfloat16
                    )

        edges = leaving.shape[2]
        select[batch, pl.ds(edges, rows)] = own_adj[batch]
        crossed[batch] = side_adj[batch].astype(jnp.float32).T.astype(jnp.bfloat16)
        initial = features[batch_range(batch), :]

        @pl.when(seg == 0)
        def _():
            entering[batch] = initial

        lookup = selector(hist_ids[pl.ds(batch, 1), :], history.shape[1])
        for slot in range(kept):
            looked = jnp.dot(
                lookup, history[slot], preferred_element_type=jnp.float32
            ).astype(jnp.bfloat16)
            past = transposed_dot(hist_adj[batch], looked)
            base[slot, batch] = (1.0 - ALPHA) * past + ALPHA * initial.astype(jnp.float32)
        return carry

    def layer(slot, batch):
        strength = jnp.float32(0.0)
        for number in range(layer_total):
            value = math.log(LAMBDA / (number + 1.0) + 1.0)
            strength = jnp.where(first_layer + slot == number, jnp.float32(value), strength)
        for direction in range(len(OFFSETS)):

            @pl.when(receives(direction))
            def _():
                edge_copy(slot, batch, direction).wait_recv()

        received = jnp.dot(
            crossed[batch], arrived[slot, batch], preferred_element_type=jnp.float32
        )
        support = (1.0 - ALPHA) * received + base[slot, batch]
        mixing = jnp.dot(
            support.astype(jnp.bfloat16), full[side, slot], preferred_element_type=jnp.float32
        )
        result = jnp.maximum((1.0 - strength) * support + strength * mixing, 0.0)
        result = result.astype(jnp.bfloat16)
        made[slot, batch_range(batch), :] = result
        store(slot, batch).start()
        if slot < kept - 1:
            send_edges(slot + 1, batch, result)
        else:

            @pl.when(seg < segments - 1)
            def _():
                hop(batch).start()

    far = chips - 1

    def line_steps(slot):
        steps = []
        for distance in range(1, chips):
            work = [(relay, (slot, distance))]
            if distance == max(1, far - 1) and slot < kept - 1:
                work.append((open_slot, (slot + 1,)))
            if distance > 1:
                work.append((bridge, (slot, distance - 1)))
            steps.append(work)
        steps.append([(bridge, (slot, far))])
        return steps

    def run(work):
        for action, arguments in work:
            if action is bridge:

                @pl.when(side == 0)
                def _():
                    action(*arguments)

            else:
                action(*arguments)

    open_slot(0)
    for load in loads:
        load.wait()

    def ready(batch, carry):
        prepare(batch, carry)

        @pl.when(seg == 0)
        def _():
            send_edges(0, batch, entering[batch])

        return carry

    def make_ready(share):
        low, high = batches * share // (far + 1), batches * (share + 1) // (far + 1)
        lax.fori_loop(low, high, ready, 0)

    make_ready(0)
    for number, work in enumerate(line_steps(0)):
        if number == far and kept > 1:
            relay(1, 1)
        run(work)
        if number < far:
            make_ready(number + 1)
    first_tasks = [[] for _ in range(batches * kept)]
    others = []
    for slot in range(1, kept):
        steps = line_steps(slot)
        if slot == 1:
            steps[0] = steps[0][1:]
            steps = [steps[0] + steps[1]] + steps[2:] if far > 1 else steps
        others += steps
        for number, work in enumerate(steps):
            first_tasks[min((slot - 1) * batches + number, slot * batches - 1)] += work

    @pl.when(seg > 0)
    def _():
        for number, work in enumerate(others):
            run(work)
            if number == 0:

                @pl.when(side == 1)
                def _():
                    open_whole(0)

    @pl.when(side == 1)
    def _():
        if not others:
            open_whole(0)
        for slot in range(kept):
            for distance in range(1, chips):
                relay_whole(slot, distance)
                if slot < kept - 1 and distance == max(1, far - 1):
                    open_whole(slot + 1)

    lag = jnp.where(seg == 0, batches, 1)
    ticks = batches + lag * (kept - 1)

    def tick(time, carry):
        @pl.when(jnp.logical_and(seg > 0, time < batches))
        def _():
            hop(time).wait_recv()
            send_edges(0, time, entering[time])

        for number, work in enumerate(first_tasks):
            if work:

                @pl.when(jnp.logical_and(seg == 0, time == number))
                def _():
                    run(work)

        for slot in range(kept - 1, -1, -1):

            @pl.when(time == lag * slot)
            def _():
                close_slot(slot)

            batch = time - lag * slot

            @pl.when(jnp.logical_and(batch >= 0, batch < batches))
            def _():
                layer(slot, batch)

        return carry

    lax.fori_loop(0, ticks, tick, 0)

    def finish(batch, carry):
        for slot in range(kept):
            store(slot, batch).wait()
            for direction in range(len(OFFSETS)):

                @pl.when(sends(direction))
                def _():
                    edge_copy(slot, batch, direction).wait_send()

        @pl.when(seg < segments - 1)
        def _():
            hop(batch).wait_send()

        return carry

    lax.fori_loop(0, batches, finish, 0)

    def drain(other, carry):
        owner = 2 * other + core
        for slot in range(kept):
            block = held(0, slot, owner, side)

            @pl.when(jnp.logical_and(other <= chip, chip < chips - 1))
            def _():
                along(slot, block, owner, 1, up_send).wait_send()

                @pl.when(side == 1)
                def _():
                    along_whole(slot, whole_shard(slot), owner, 1, up_whole).wait_send()

            @pl.when(jnp.logical_and(other >= chip, chip > 0))
            def _():
                along(slot, block, owner, -1, down_send).wait_send()

                @pl.when(side == 1)
                def _():
                    along_whole(slot, whole_shard(slot), owner, -1, down_whole).wait_send()

            @pl.when(other != chip)
            def _():
                @pl.when(side == 0)
                def _():
                    for which in range(2):
                        to_pair(slot, owner, which).wait_send()

                @pl.when(side == 1)
                def _():
                    to_mate(slot, owner).wait_send()
                    whole_to_pair(slot, owner).wait_send()

            @pl.when(other == chip)
            def _():
                shard_to_pair(slot, whole_shard(slot), owner).wait_send()

        return carry

    lax.fori_loop(0, chips, drain, 0)


def staged(features, weights, history, own_adj, side_adj, hist_adj, send_ids, hist_ids):
    segments = lax.axis_size("segment")
    places = lax.axis_size("graph")
    layer_total, shard, width = weights.shape
    kept = layer_total // segments
    batches, rows = own_adj.shape[0], own_adj.shape[2]
    edges = side_adj.shape[1] * side_adj.shape[2]
    chips = places // 2
    dma = pltpu.SemaphoreType.DMA

    def kernel(*refs):
        stage_kernel(segments, places, layer_total, *refs)

    anywhere = pl.BlockSpec(memory_space=pl.ANY)
    half = jnp.bfloat16
    return pl.pallas_call(
        kernel,
        out_shape=jax.ShapeDtypeStruct((kept, batches * rows, width), half),
        in_specs=[anywhere] * 8,
        out_specs=anywhere,
        scratch_shapes=[
            pltpu.VMEM(features.shape, half),
            pltpu.VMEM((kept,) + history.shape[1:], half),
            pltpu.VMEM(own_adj.shape, half),
            pltpu.VMEM((batches, edges, rows), half),
            pltpu.VMEM(hist_adj.shape, half),
            pltpu.VMEM(send_ids.shape, send_ids.dtype),
            pltpu.VMEM(hist_ids.shape, hist_ids.dtype),
            pltpu.VMEM((kept, batches * rows, width), half),
            pltpu.VMEM((2, kept, places * shard, width), half),
            pltpu.VMEM((kept, batches, rows, width), jnp.float32),
            pltpu.VMEM((batches, edges + rows, rows), half),
            pltpu.VMEM((batches, rows, edges), half),
            pltpu.VMEM((batches, rows, width), half),
            pltpu.VMEM((kept, batches, edges, width), half),
            pltpu.VMEM((kept, batches, edges, width), half),
            dma((7,)),
            dma((kept,)),
            dma((kept, batches)),
            dma((2, kept, chips)),
            dma((kept, chips)),
            dma((kept, 2, chips)),
            dma((kept,)),
            dma((kept, chips)),
            dma((kept, chips)),
            dma((kept, chips)),
            dma((kept, chips)),
            dma((kept, chips)),
            dma((kept, 2, chips)),
            dma((kept,)),
            dma((kept, batches, len(OFFSETS))),
            dma((kept, batches, len(OFFSETS))),
            dma((batches,)),
            dma((batches,)),
        ],
        compiler_params=pltpu.CompilerParams(
            collective_id=0, has_side_effects=True, vmem_limit_bytes=60 * 1024 * 1024
        ),
    )(
        features,
        weights,
        history,
        own_adj,
        side_adj.reshape(batches, edges, rows),
        hist_adj,
        send_ids,
        hist_ids,
    )


def device_part(features, weights, *rest):
    places, segments = lax.axis_size("graph"), lax.axis_size("segment")
    whole_tiles = weights.shape[1] % (2 * TILE_ROWS) == 0 and rest[2].shape[2] % TILE_ROWS == 0
    even = places % 2 == 0 and segments % 2 == 0 and weights.shape[0] % segments == 0
    if whole_tiles and even:
        return staged(features, weights, *rest)
    return shards(features, weights, *rest)


def solution(mesh):
    in_specs = (
        P("graph", None),
        P(None, "graph", None),
        P(None, "graph", None),
        P(None, "graph", None),
        P(None, None, "graph", None),
        P(None, "graph", None),
        P(None, None, "graph"),
        P(None, "graph"),
    )
    out_specs = P("segment", "graph", None)
    return jax.shard_map(device_part, mesh=mesh, in_specs=in_specs, out_specs=out_specs, check_vma=False)
```
